512 devices in a mesh: sub: 128 (over y, z, core), col: 4 (over x).
Axes of the slice: x: 4, y: 8, z: 8, core: 2. Of those that a mesh axis runs over, the one named last changes fastest.
Arguments:
- sep_q: bfloat16 [128, 512, 56], P('sub', 'col'), may hold values from -6 to 6
- sep_phi: bfloat16 [128, 8, 4064], P('sub'), may hold values from -0.5 to 0.5
- separator_constraint_coupling: bfloat16 [128, 328704], P('sub'), may hold values from -0.09375 to 0.09375
- leaf_q: bfloat16 [128, 512, 128], P('sub', 'col'), may hold values from -6 to 6
- leaf_phi: bfloat16 [128, 128, 640], P('sub'), may hold values from -0.5 to 0.5
- leaf_coupling: bfloat16 [128, 4064, 640], P('sub', 'col'), may hold values from -0.09375 to 0.09375
- leaf_interior_rows: int32 [128], P('sub'), may hold values from 1 to 640, 61440 in all
Outputs:
- sep_values: bfloat16 [128, 512, 112], P('sub', 'col')
- leaf_recovered_values: bfloat16 [128, 512, 640], P('sub', 'col')
The draws below stay inside these ranges and needn't reach their ends.
Inputs may be any that keep to these rules, and one draw needn't show every extreme that they name: `leaf_interior_rows`: the live rows of all leaves sum to 61440, and some leaf has exactly 640.
All inputs are finite; a program needn't handle non-finite values. No bound on the sum of `leaf_interior_rows` on one device may be relied on, other than what follows from the above.
Results may differ from the reference program's by a relative error of at most 0.0044.
Values may be sent and summed in bfloat16 or wider, within the bound.
A program may use at most 64 MiB of HBM per device.

```python
import math
import jax
import jax.numpy as jnp
import numpy as np
from jax import lax

COLS = 512
SMODE = 8
LMODE = 128
SEP_DEV = 16
LEAF = 640
SUBS = 128
LEVELS = 7
ANC = 4064
CPL = 328704


def draw_sep_phi(key, part):
    key = jax.random.fold_in(key, 11)
    table = np.zeros((ANC,), np.float32)
    for slot in range(LEVELS):
        group = SUBS // 2 ** slot
        start = SEP_DEV * (2 * SUBS - 2 * group)
        table[start:start + SEP_DEV * group] = 1.0 / np.sqrt(SMODE * group)
    raw = jnp.clip(jax.random.normal(key, (SUBS, SMODE, ANC), jnp.float32), -2.0, 2.0)
    return (raw * jnp.asarray(table)[None, None, :]).astype(jnp.bfloat16)


def levels(own_key, dims, pieces, smallest, high):
    level, own = 1.0, jax.random.fold_in(own_key, 6)
    for position, parts in pieces:
        heights = jnp.exp(jax.random.uniform(jax.random.fold_in(own, position), (parts,), jnp.float32, smallest / len(pieces), high / len(pieces)))
        level = level * jnp.repeat(heights, dims[position] // parts).reshape([-1 if axis == position else 1 for axis in range(len(dims))])
    return level


def length_profile(count, total, limit, lean):
    portions = [(1 << 20) // math.isqrt(standing ** lean) + 1 for standing in range(2, count + 1)]
    surplus, holding = total - limit - (count - 1), [1] * (count - 1)
    while surplus > 0:
        free = [i for i in range(count - 1) if holding[i] < limit]
        whole, remaining = sum([portions[i] for i in free]), surplus
        for i in free:
            more = min(limit - holding[i], max(1, remaining * portions[i] // whole), surplus)
            holding[i] = holding[i] + more
            surplus = surplus - more
    return np.array([limit] + holding)


def ragged_sizes(rng, amount, total, reach, slope):
    if amount == 2:
        one = jax.random.randint(rng, (), max(1, total - reach), min(reach, total - 1) + 1)
        return jnp.stack([one, total - one])
    lengths = jnp.asarray(length_profile(amount, total, reach, slope), jnp.int32)
    pairs = (amount - 1) // 2
    donor, taker = lengths[1:1 + 2 * pairs:2], lengths[2:2 + 2 * pairs:2]
    slack = jnp.minimum(donor - 1, reach - taker)
    shifted = jax.random.randint(jax.random.fold_in(rng, 1), (pairs,), 0, 1 << 20) % (slack + 1)
    lengths = lengths.at[1:1 + 2 * pairs:2].set(donor - shifted).at[2:2 + 2 * pairs:2].set(taker + shifted)
    return lengths[jax.random.permutation(jax.random.fold_in(rng, 2), amount)]


def normal_values(stream_key, shape, scale, most, shards=(), kind=jnp.bfloat16):
    result = scale * jax.random.normal(stream_key, shape, jnp.float32)
    if shards:
        result = result * levels(stream_key, shape, shards, -0.22, 0.18)
    return jnp.clip(result, -most, most).astype(kind)


def setup_inputs(seed: int = 0) -> dict:
    key_list = jax.random.split(jax.random.key(seed), 8)
    return {
        "sep_q": normal_values(key_list[0], (SUBS, COLS, LEVELS * SMODE), 1.0, 6.0, ((0, 128), (1, 4))),
        "sep_phi": draw_sep_phi(jax.random.fold_in(key_list[7], 71), 0),
        "separator_constraint_coupling": normal_values(key_list[2], (SUBS, CPL), ANC ** -0.5, 0.09375, ((0, 128),)),
        "leaf_q": normal_values(key_list[3], (SUBS, COLS, LMODE), 1.0, 6.0, ((0, 128), (1, 4))),
        "leaf_phi": normal_values(key_list[4], (SUBS, LMODE, LEAF), LMODE ** -0.5, 0.5, ((0, 128),)),
        "leaf_coupling": normal_values(key_list[5], (SUBS, ANC, LEAF), ANC ** -0.5, 0.09375, ((0, 128), (1, 4))),
        "leaf_interior_rows": ragged_sizes(key_list[6], SUBS, SUBS * LEAF * 3 // 4, LEAF, 1).astype(jnp.int32),
    }


def reference(sep_q, sep_phi, separator_constraint_coupling, leaf_q, leaf_phi, leaf_coupling, leaf_interior_rows):
    single_precision = jnp.float32
    values = []
    groups = []
    shares = []
    coff = 0
    for slot in range(LEVELS):
        group = SUBS // (2 ** slot)
        start = SEP_DEV * (2 * SUBS - 2 * group)
        width = SEP_DEV * group
        count = SUBS // group
        modal_amplitudes = sep_q[:, :, slot * SMODE:(slot + 1) * SMODE].reshape(count, group, COLS, SMODE)
        modal_amplitudes = modal_amplitudes.transpose(0, 2, 1, 3).reshape(count, COLS, group * SMODE)
        separator_phis = sep_phi[:, :, start:start + width].reshape(count, group * SMODE, width)
        modal_matrix = jnp.einsum("qwb,qbo->qwo", modal_amplitudes.astype(single_precision), separator_phis.astype(single_precision))
        couple = jnp.zeros((SUBS, COLS, SEP_DEV), single_precision)
        if slot > 0:
            block = separator_constraint_coupling[:, coff:coff + start * SEP_DEV].reshape(SUBS, start, SEP_DEV)
            first = 0
            for earlier in range(slot):
                g2 = groups[earlier]
                w2 = SEP_DEV * g2
                piece = block[:, first:first + w2].reshape(SUBS // g2, g2, w2, SEP_DEV)
                term = jnp.einsum("xca,xeat->xect", values[earlier].astype(single_precision), piece.astype(single_precision))
                couple = couple + term.reshape(SUBS, COLS, SEP_DEV)
                first = first + w2
        coff = coff + start * SEP_DEV
        couple = couple.reshape(count, group, COLS, SEP_DEV).transpose(0, 2, 1, 3).reshape(count, COLS, width)
        value = (modal_matrix + couple).astype(jnp.bfloat16)
        values.append(value)
        groups.append(group)
        share = value.reshape(count, COLS, group, SEP_DEV).transpose(0, 2, 1, 3).reshape(SUBS, COLS, SEP_DEV)
        shares.append(share)

    def one_leaf(index):
        known = jnp.concatenate([values[s][index // groups[s]] for s in range(LEVELS)], axis=1)
        total = jnp.dot(leaf_q[index], leaf_phi[index], preferred_element_type=jnp.float32)
        total = total + jnp.dot(known, leaf_coupling[index], preferred_element_type=jnp.float32)
        live = jnp.arange(LEAF, dtype=jnp.int32)[None, :] < leaf_interior_rows[index]
        return jnp.where(live, total, jnp.float32(0.0)).astype(jnp.bfloat16)

    leaf_recovered_values = lax.map(one_leaf, jnp.arange(SUBS, dtype=jnp.int32))
    return jnp.concatenate(shares, axis=2), leaf_recovered_values
```

```python
import jax
import jax.numpy as jnp
from jax import lax
from jax.experimental import pallas as pl
from jax.experimental.pallas import tpu as pltpu
from jax.sharding import PartitionSpec as P

MESH = pl.DeviceIdType.MESH
F32 = jnp.float32
BF16 = jnp.bfloat16
NY, NZ, NC, NX = 8, 8, 2, 4
COLS = 128
LEAF = 640
GROUPS = ((8, 8), (4, 8), (2, 8), (1, 8), (1, 4), (1, 2), (1, 1))
LEVELS = len(GROUPS)
OFF = (0, 2048, 3072, 3584, 3840, 3968, 4032)
CROW = (0, 0, 256, 640, 1088, 1568, 2064)
CHUNKS = (0, 2, 3, 4, 4, 4, 4)
NEAR = 3072
CROWS = 2568


def dot_t(a, b):
    return lax.dot_general(a, b, (((0,), (0,)), ((), ())), preferred_element_type=F32)


def dot(a, b):
    return jnp.dot(a, b, preferred_element_type=F32)


def kernel(
    q_ref, phi_ref, c_hbm, lq_ref, lphi_ref, cpl_hbm, rows_ref,
    sv_ref, out_ref,
    c_flat, c_rows, spread, select, xt, cpl, cps, tail2, tail3,
    ms, mr, qs, qr, bs, br0, br1, br2, m3, m456,
    cl3, cl4, cl5, cl6, pp3, pp4, pp5, pp6,
    k0, k1, k2, k3, k4, k5, k6, pv, acc, kxm, kxe, ps, pr,
    sems,
):
    known = (k0, k1, k2)
    sub = lax.axis_index("sub")
    x = lax.axis_index("col")
    y, z, c = sub // 16, (sub // 2) % 8, sub % 2
    other = 1 - c
    zc = z * 2 + c
    zq = (z % 4) * 2 + c

    counter = [0]

    def new_sems(n):
        first = counter[0]
        counter[0] += n
        return [sems.at[first + i] for i in range(n)]

    def dev(y_, z_, c_):
        return ((y_ * 8 + z_) * 2 + c_, x)

    def send(src, dst, ss, rs, target):
        pltpu.make_async_remote_copy(
            src_ref=src, dst_ref=dst, send_sem=ss, recv_sem=rs,
            device_id=target, device_id_type=MESH,
        ).start()

    def drain(like, sem):
        pltpu.make_async_copy(like, like, sem).wait()

    drains = []

    (c_sem, cpl_sem) = new_sems(2)
    c_copy = pltpu.make_async_copy(c_hbm, c_flat, c_sem)
    c_copy.start()
    cpl_copy = pltpu.make_async_copy(cpl_hbm, cpl, cpl_sem)
    cpl_copy.start()

    barrier = pltpu.get_barrier_semaphore()
    for k in range(1, 16):
        d = (zc + k) % 16
        pl.semaphore_signal(barrier, inc=1, device_id=dev(y, d // 2, d % 2), device_id_type=MESH)
    half, pair = (y // 4) * 4, (y // 2) * 2
    mate = 2 * pair + 1 - y
    for k in range(1, 4):
        for i in range(NZ):
            pl.semaphore_signal(barrier, inc=1, device_id=dev(half + (y + k) % 4, i, c), device_id_type=MESH)
    for i in range(NZ):
        pl.semaphore_signal(barrier, inc=1, device_id=dev(mate, i, other), device_id_type=MESH)
    for k in range(4):
        pl.semaphore_signal(barrier, inc=1, device_id=dev(4 - half + k, z, c), device_id_type=MESH)
    for k in range(1, NX):
        pl.semaphore_signal(barrier, inc=1, device_id=(sub, (x + k) % NX), device_id_type=MESH)

    phi = phi_ref[...].astype(F32)
    qf = q_ref[...].astype(F32)
    lane = lax.broadcasted_iota(jnp.int32, (8, 128), 1)
    for d in range(16):
        h, p = divmod(d, 8)
        parts = [qf[0:32]]
        for g in range(2):
            piece = jnp.zeros((8, 128), F32)
            for b in range(8 * g, min(8 * g + 8, 15)):
                block = phi[:, b * 256 + h * 128 : b * 256 + h * 128 + 128]
                shift = ((b % 8 - p) * 16) % 128
                if shift:
                    block = pltpu.roll(block, shift, 1)
                piece = jnp.where(lax.shift_right_logical(lane, 4) == b % 8, block, piece)
            parts.append(piece)
        ms[d] = jnp.concatenate(parts, axis=0).astype(BF16)
    qs[...] = jnp.concatenate(
        [
            qf[32:56],
            phi[:, 3840:3968],
            jnp.concatenate([phi[:, 3968:4064], jnp.zeros((8, 32), F32)], axis=1),
            jnp.zeros((8, 128), F32),
        ],
        axis=0,
    ).astype(BF16)
    mr[zc] = ms[zc]
    qr[zq] = qs[...]
    pr[x] = jnp.zeros((COLS, LEAF), BF16)

    pl.semaphore_wait(barrier, 15 + 24 + 8 + 4 + NX - 1)

    (a_send, a_recv, q_send, q_recv) = new_sems(4)
    for k in range(1, 16):
        d = (zc + k) % 16
        send(ms.at[d], mr.at[zc], a_send, a_recv, dev(y, d // 2, d % 2))
    for k in range(1, 8):
        d = (zq + k) % 8
        send(qs, qr.at[zq], q_send, q_recv, dev(y, (z // 4) * 4 + d // 2, d % 2))
    drains.append(lambda: drain(mr.at[pl.ds(0, 15)], a_send))
    drains.append(lambda: drain(qr.at[pl.ds(0, 7)], q_send))

    (t_send, f_send, t2_recv, ta_recv, tb_recv) = new_sems(5)
    tail_a, tail_b = tail3.at[pl.ds(0, 512)], tail3.at[pl.ds(512, 512)]
    cpl_copy.wait()

    @pl.when(x == 2)
    def _():
        tail2[0:480] = cpl[528:1008]
        tail2[480:512] = jnp.concatenate([cpl[1008:1016], jnp.zeros((24, LEAF), BF16)], axis=0)
        send(tail2, tail2, t_send, t2_recv, (sub, 1))
        send(tail2, tail2, t_send, t2_recv, (sub, 3))

    @pl.when(x == 3)
    def _():
        tail3[0:992] = cpl[24:1016]
        tail3[992:1024] = jnp.concatenate([jnp.zeros((8, LEAF), BF16), cpl[0:24]], axis=0)
        send(tail_a, tail_a, t_send, ta_recv, (sub, 0))
        send(tail_b, tail_b, t_send, tb_recv, (sub, 2))
        send(tail_b, tail_b, t_send, tb_recv, (sub, 0))
        send(tail_a, tail_a, t_send, ta_recv, (sub, 2))

    def pass_on():
        @pl.when(x == 0)
        def _():
            drain(tail_a, ta_recv)
            send(tail_a, tail_a, f_send, ta_recv, (sub, 1))

        @pl.when(x == 1)
        def _():
            drain(tail2, t2_recv)
            send(tail2, tail2, f_send, t2_recv, (sub, 0))

        @pl.when(x == 2)
        def _():
            drain(tail_b, tb_recv)
            send(tail_b, tail_b, f_send, tb_recv, (sub, 1))

    def finish_tail():
        @pl.when(x == 2)
        def _():
            drain(tail2, t_send)
            drain(tail2, t_send)

        @pl.when(x == 3)
        def _():
            drain(tail3, t_send)
            drain(tail3, t_send)

        @pl.when(x < 3)
        def _():
            drain(tail2, f_send)

    drains.append(finish_tail)

    c_copy.wait()
    wide_row = lax.broadcasted_iota(jnp.int32, (128, 1024), 0)
    wide_col = lax.broadcasted_iota(jnp.int32, (128, 1024), 1)
    spread[...] = jnp.where(lax.shift_right_logical(wide_col, 3) == wide_row, 1.0, 0.0).astype(BF16)
    select[...] = jnp.where((wide_col & 7) == lax.shift_right_logical(wide_row, 4), 1.0, 0.0)

    def rows_of(s):
        steps, each = ((0, 0), (4, 8), (6, 8), (8, 8), (8, 8), (8, 8), (7, 9))[s]

        def step(i, carry):
            for k in range(each):
                row = pl.multiple_of(CROW[s] + (i * each + k) * 8, 8)
                at = pl.multiple_of(row * 128, 1024)
                value = c_flat[0:1, pl.ds(at, 1024)].astype(F32).reshape(8, 128)
                c_rows[pl.ds(row, 8), :] = value
            return carry

        lax.fori_loop(0, steps, step, 0)
        if s == LEVELS - 1:
            c_rows[CROWS : CROWS + 8, :] = jnp.zeros((8, 128), F32)

    def expand(s):
        rows_of(s)

        def step(i, carry):
            rows = c_rows[pl.ds(pl.multiple_of(CROW[s] + i * 128, 8), 128), :].astype(BF16)
            wide = dot_t(rows, spread[...]) * select[...]
            xt[s - 1, :, pl.ds(pl.multiple_of(i * 1024, 1024), 1024)] = wide.astype(BF16)
            return carry

        lax.fori_loop(0, CHUNKS[s], step, 0)

    expand(1)
    expand(2)

    drain(mr.at[pl.ds(0, 15)], a_recv)
    got = mr[...].astype(F32)
    coords = [got[:, 8 * s : 8 * s + 8].reshape(128, 128).astype(BF16) for s in range(4)]
    shapes_lo = got[:, 32:40].reshape(128, 128).astype(BF16)
    shapes_hi = got[:, 40:48].reshape(128, 128).astype(BF16)
    bs[0:8] = dot_t(shapes_lo, coords[0]).reshape(8, 16, 128)
    (b0_send, b0_recv, b1_send, b1_recv, b2_send, b2_recv) = new_sems(6)
    br0[y] = bs[y]
    for k in range(1, NY):
        d = (y + k) % NY
        send(bs.at[d], br0.at[y], b0_send, b0_recv, dev(d, z, c))
    drains.append(lambda: drain(br0.at[pl.ds(0, 7)], b0_send))
    bs[8:12] = dot_t(shapes_hi, coords[1])[0:64].reshape(4, 16, 128)
    br1[y % 4] = bs[8 + y % 4]
    for k in range(1, 4):
        d = (y % 4 + k) % 4
        send(bs.at[8 + d], br1.at[y % 4], b1_send, b1_recv, dev((y // 4) * 4 + d, z, c))
    drains.append(lambda: drain(br1.at[pl.ds(0, 3)], b1_send))
    bs[12:14] = dot_t(shapes_hi, coords[2])[64:96].reshape(2, 16, 128)
    br2[y % 2] = bs[12 + y % 2]
    d = 1 - y % 2
    send(bs.at[12 + d], br2.at[y % 2], b2_send, b2_recv, dev((y // 2) * 2 + d, z, c))
    drains.append(lambda: drain(br2.at[0], b2_send))
    m3[...] = dot_t(shapes_hi, coords[3])[96:112]

    expand(3)

    def publish(s, modal, product):
        if product is not None:
            modal = modal + jnp.sum(product.reshape(8, 16, 128), axis=0)
        value = modal.astype(BF16)
        ny, nz = GROUPS[s]
        known[s][y % ny, z % nz, c] = value
        sv_ref[16 * s : 16 * s + 16, :] = value

    def block_rows(s):
        ny, nz = GROUPS[s]
        return known[s][...].reshape(ny * nz * 32, 128)

    def critical(s):
        width = OFF[s] - OFF[s - 1]
        product = dot(xt[s - 1, :, OFF[s - 1] : OFF[s - 1] + width], block_rows(s - 1))
        if s >= 2:
            product = product + pv[s - 2]
        return product

    def ahead(r):
        count = LEVELS - 2 - r
        width = OFF[r + 1] - OFF[r]
        lhs = xt[r + 1 : LEVELS - 1, :, OFF[r] : OFF[r] + width].reshape(count * 128, width)
        value = dot(lhs, block_rows(r)).reshape(count, 128, 128)
        if r == 0:
            pv[...] = value
        else:
            pv[r:] = pv[r:] + value

    def spread_wide(s, during_first, during_second):
        ny, nz = GROUPS[s]
        k_ref = known[s]
        yi, zi = y % ny, z % nz
        y0, z0 = y - yi, z - zi
        (s1, r1, s2, s3, r3) = new_sems(5)
        r2 = new_sems(max(ny, nz) - 1)

        @pl.when(c == 0)
        def _():
            for k in range(1, ny):
                own = k_ref.at[yi, zi, 0]
                send(own, own, s1, r1, dev(y0 + (yi + k) % ny, z, 0))

        @pl.when(c == 1)
        def _():
            for k in range(1, nz):
                own = k_ref.at[yi, zi, 1]
                send(own, own, s1, r1, dev(y, z0 + (zi + k) % nz, 1))

        during_first()

        @pl.when(c == 0)
        def _():
            drain(k_ref.at[pl.ds(0, ny - 1), 0, 0], r1)
            own = k_ref.at[:, zi, 0]
            for k in range(1, nz):
                send(own, own, s2, r2[k - 1], dev(y, z0 + (zi + k) % nz, 0))
            send(own, own, s3, r3, dev(y, z, 1))

        @pl.when(c == 1)
        def _():
            drain(k_ref.at[0, pl.ds(0, nz - 1), 0], r1)
            own = k_ref.at[yi, :, 1]
            for k in range(1, ny):
                send(own, own, s2, r2[k - 1], dev(y0 + (yi + k) % ny, z, 1))
            send(own, own, s3, r3, dev(y, z, 0))

        during_second()

        def nearest(n):
            return sorted(range(1, n), key=lambda k: (min(k, n - k), k))

        @pl.when(c == 0)
        def _():
            for k in nearest(nz):
                piece = k_ref.at[:, (zi + nz - k) % nz, 0]
                drain(piece, r2[k - 1])
                send(piece, piece, s3, r3, dev(y, z, 1))

        @pl.when(c == 1)
        def _():
            for k in nearest(ny):
                piece = k_ref.at[(yi + ny - k) % ny, :, 1]
                drain(piece, r2[k - 1])
                send(piece, piece, s3, r3, dev(y, z, 0))

        drain(k_ref.at[:, :, 0], r3)

        def finish():
            @pl.when(c == 0)
            def _():
                drain(k_ref.at[pl.ds(0, ny - 1), 0, 0], s1)
                drain(k_ref.at[:, pl.ds(0, nz - 1), 0], s2)

            @pl.when(c == 1)
            def _():
                drain(k_ref.at[0, pl.ds(0, nz - 1), 0], s1)
                drain(k_ref.at[pl.ds(0, ny - 1), :, 0], s2)

            drain(k_ref.at[:, :, 0], s3)

        drains.append(finish)

    def spread_half(during):
        yi = y % 4
        (s0, s1, s3, r3) = new_sems(4)
        r1 = new_sems(4)
        own = k1.at[yi, z, c]
        for k in range(4):
            for i in range(1 if k == 0 else 0, NZ):
                send(own, own, s1 if k else s0, r1[k], dev(half + (y + k) % 4, (z + i) % NZ, c))
        during()
        drain(k1.at[0, pl.ds(0, 7), 0], r1[0])
        for k in (0, 1, 3, 2):
            piece = k1.at[(yi + 4 - k) % 4, :, c]
            if k:
                drain(piece, r1[k])
            send(piece, piece, s3, r3, dev(y, z, other))
        drain(k1.at[:, :, 0], r3)

        def finish():
            drain(k1.at[0, pl.ds(0, 7), 0], s0)
            drain(k1.at[pl.ds(0, 3), :, 0], s1)
            drain(k1.at[:, :, 0], s3)

        drains.append(finish)

    def spread_pair(during):
        (s0, s1, r0, r1) = new_sems(4)
        own = k2.at[y % 2, z, c]
        for k in range(16):
            d = (zc + k) % 16
            send(own, own, s1, r1, dev(mate, d // 2, d % 2))
            if k:
                send(own, own, s0, r0, dev(y, d // 2, d % 2))
        during()
        drain(k0.at[pl.ds(0, 5), pl.ds(0, 3), 0], r0)
        drain(k0.at[pl.ds(0, 4), pl.ds(0, 4), 0], r1)

        def finish():
            drain(k0.at[pl.ds(0, 5), pl.ds(0, 3), 0], s0)
            drain(k0.at[pl.ds(0, 4), pl.ds(0, 4), 0], s1)

        drains.append(finish)

    (xm, xe, p_recv) = new_sems(3)

    def x_send(src, dst, rs, d):
        (ss,) = new_sems(1)

        @pl.when(x != d)
        def _():
            send(src, dst, ss, rs, (sub, d))

        def finish():
            @pl.when(x != d)
            def _():
                drain(src, ss)

        drains.append(finish)

    def stage():
        zeros = jnp.zeros((16, LEAF), BF16)

        @pl.when(x == 0)
        def _():
            cps[0:1008] = cpl[0:1008]
            cps[1008:1024] = jnp.concatenate([cpl[1008:1016], zeros[0:8]], axis=0)

        @pl.when(x == 1)
        def _():
            cps[0:1008] = cpl[8:1016]
            cps[1008:1024] = zeros
            cps[1024:1040] = jnp.concatenate([zeros[0:8], cpl[0:8]], axis=0)

        @pl.when(x == 2)
        def _():
            cps[0:512] = cpl[16:528]
            cps[1024:1040] = cpl[0:16]

        acc[...] = dot(lq_ref[...], lphi_ref[...])

    def partial(xs):
        sends = new_sems(4)

        @pl.when(x == xs)
        def _():
            if xs < 2:
                drain(kxm.at[pl.ds(0, 3)], xm)
            else:
                drain(kxm.at[pl.ds(0, 3), pl.ds(0, 2)], xm)
            if xs:
                drain(kxe.at[pl.ds(0, 3)], xe)
            for p in range(NX):
                mine = p == xs
                if xs == 0:
                    main = (k0[0:4] if mine else kxm[p]).reshape(1024, 128)
                    extra = None
                elif xs == 1:
                    main = (k0[4:8] if mine else kxm[p]).reshape(1024, 128)
                    extra = k0[3, 7, 1] if mine else kxe[p]
                else:
                    main = (k1[0:2] if mine else kxm[p, 0:2]).reshape(512, 128)
                    extra = k0[7, 7, 1] if mine else kxe[p]
                value = dot_t(main, cps[0 : main.shape[0]])
                if extra is not None:
                    value = value + dot_t(extra, cps[1024 : 1024 + extra.shape[0]])
                if mine:
                    acc[...] += value
                else:
                    ps[p] = value.astype(BF16)
                    send(ps.at[p], pr.at[xs], sends[p], p_recv, (sub, p))

        def finish():
            @pl.when(x == xs)
            def _():
                for p in range(NX):
                    if p != xs:
                        drain(ps.at[p], sends[p])

        drains.append(finish)

    drain(br0.at[pl.ds(0, 7)], b0_recv)
    publish(0, jnp.sum(br0[...], axis=0), None)

    def second_0():
        pass_on()
        expand(5)

    spread_wide(0, lambda: expand(4), second_0)

    drain(br1.at[pl.ds(0, 3)], b1_recv)
    publish(1, jnp.sum(br1[...], axis=0), critical(1))

    (c3_send, c3_recv, c4_send, c4_recv, c5_send, c5_recv, c6_send, c6_recv) = new_sems(8)
    (p3_send, p3_recv, p4_send, p4_recv, p5_send, p5_recv, p6_send, p6_recv) = new_sems(8)
    near4, near5, near6 = zq, zq % 4, c

    def to_near(b3, b4, b5, b6, sems_):
        s3, r3, s4, r4, s5, r5, s6, r6 = sems_
        for k in range(1, 16):
            d = (zc + k) % 16
            send(b3.at[zc], b3.at[zc], s3, r3, dev(y, d // 2, d % 2))
        for k in range(1, 8):
            d = (near4 + k) % 8
            send(b4.at[near4], b4.at[near4], s4, r4, dev(y, (z // 4) * 4 + d // 2, d % 2))
        for k in range(1, 4):
            d = (near5 + k) % 4
            send(b5.at[near5], b5.at[near5], s5, r5, dev(y, (z // 2) * 2 + d // 2, d % 2))
        send(b6.at[near6], b6.at[near6], s6, r6, dev(y, z, other))

        def finish():
            drain(b3.at[pl.ds(0, 15)], s3)
            drain(b4.at[pl.ds(0, 7)], s4)
            drain(b5.at[pl.ds(0, 3)], s5)
            drain(b6.at[0], s6)

        drains.append(finish)

    def during_1():
        x_send(k0.at[pl.ds(0, 4)], kxm.at[x], xm, 0)
        x_send(k0.at[pl.ds(4, 4)], kxm.at[x], xm, 1)
        x_send(k0.at[3, 7, 1], kxe.at[x], xe, 1)
        x_send(k0.at[7, 7, 1], kxe.at[x], xe, 2)
        expand(6)
        ahead(0)

        def fold(s, width):
            wide = xt[s - 1, :, NEAR : NEAR + width].astype(F32)
            return jnp.sum(wide.reshape(8, 16, width), axis=0).astype(BF16)

        cl3[zc] = fold(3, 512)
        cl4[near4] = fold(4, 768)
        cl5[near5] = fold(5, 896)
        cl6[near6] = fold(6, 1024)
        to_near(cl3, cl4, cl5, cl6, (c3_send, c3_recv, c4_send, c4_recv, c5_send, c5_recv, c6_send, c6_recv))

        drain(qr.at[pl.ds(0, 7)], q_recv)
        near = qr[...].astype(F32)
        member = lax.shift_right_logical(lax.broadcasted_iota(jnp.int32, (64, 128), 0), 3)
        q4, q5, q6 = [near[:, 8 * i : 8 * i + 8].reshape(64, 128) for i in range(3)]
        q5 = jnp.where(lax.shift_right_logical(member, 2) == (z % 4) // 2, q5, 0.0)
        q6 = jnp.where(lax.shift_right_logical(member, 1) == z % 4, q6, 0.0)
        hi = near[:, 24:32].reshape(64, 128).astype(BF16)
        lo = near[:, 32:40].reshape(64, 128).astype(BF16)
        m456[0] = dot_t(hi, q4.astype(BF16))
        m456[1] = dot_t(lo, q5.astype(BF16))
        m456[2] = dot_t(lo, q6.astype(BF16))

    spread_half(during_1)

    drain(br2.at[0], b2_recv)
    publish(2, jnp.sum(br2[...], axis=0), critical(2))

    def during_2():
        ahead(1)

        def prefix(s, modal):
            return (modal + jnp.sum(pv[s - 2].reshape(8, 16, 128), axis=0)).astype(BF16)

        def own_rows(s, at):
            return m456[s - 4, pl.ds(pl.multiple_of(at, 16), 16), :]

        pp3[zc] = prefix(3, m3[...])
        pp4[near4] = prefix(4, own_rows(4, near4 * 16))
        pp5[near5] = prefix(5, own_rows(5, near5 * 16))
        pp6[near6] = prefix(6, own_rows(6, 64 + near6 * 16))
        to_near(pp3, pp4, pp5, pp6, (p3_send, p3_recv, p4_send, p4_recv, p5_send, p5_recv, p6_send, p6_recv))
        x_send(k1.at[pl.ds(0, 2)], kxm.at[x, pl.ds(0, 2)], xm, 2)
        stage()
        partial(0)
        partial(1)

        @pl.when((x == 0) | (x == 3))
        def _():
            drain(tail2, t2_recv)

        acc[...] += dot_t(k1[2:4].reshape(512, 128), tail2[...])
        partial(2)

    spread_pair(during_2)

    drain(cl3.at[pl.ds(0, 15)], c3_recv)
    drain(cl4.at[pl.ds(0, 7)], c4_recv)
    drain(cl5.at[pl.ds(0, 3)], c5_recv)
    drain(cl6.at[0], c6_recv)
    drain(pp3.at[pl.ds(0, 15)], p3_recv)
    drain(pp4.at[pl.ds(0, 7)], p4_recv)
    drain(pp5.at[pl.ds(0, 3)], p5_recv)
    drain(pp6.at[0], p6_recv)
    above2 = block_rows(2)
    c3, c4 = cl3[...].reshape(256, 512), cl4[...].reshape(128, 768)
    c5, c6 = cl5[...].reshape(64, 896), cl6[...].reshape(32, 1024)
    first = dot(jnp.concatenate([c3, c4[:, 0:512], c5[:, 0:512], c6[:, 0:512]], axis=0), above2)
    above3 = (pp3[...].reshape(256, 128).astype(F32) + first[0:256]).astype(BF16)
    second = dot(jnp.concatenate([c4[:, 512:768], c5[:, 512:768], c6[:, 512:768]], axis=0), above3) + first[256:480]
    above4 = (pp4[...].reshape(128, 128).astype(F32) + second[0:128]).astype(BF16)
    third = dot(jnp.concatenate([c5[:, 768:896], c6[:, 768:896]], axis=0), above4) + second[128:224]
    above5 = (pp5[...].reshape(64, 128).astype(F32) + third[0:64]).astype(BF16)
    above6 = pp6[...].reshape(32, 128).astype(F32) + third[64:96] + dot(c6[:, 896:960], above5)
    above6 = above6.astype(BF16)
    k3[...] = above3.reshape(16, 16, 128)
    k4[...] = above4.reshape(8, 16, 128)
    k5[...] = above5.reshape(4, 16, 128)
    k6[...] = above6.reshape(2, 16, 128)
    sv_ref[48:64, :] = k3[zc]
    sv_ref[64:80, :] = k4[near4]
    sv_ref[80:96, :] = k5[near5]
    sv_ref[96:112, :] = k6[near6]

    @pl.when(x < 2)
    def _():
        drain(tail_b, tb_recv)

    @pl.when((x == 1) | (x == 2))
    def _():
        drain(tail_a, ta_recv)

    late = jnp.concatenate([above2, above3, above4, above5, above6, k1[3, 7].reshape(32, 128)], axis=0)
    total = acc[...] + dot_t(late, tail3[...])

    @pl.when(x == 3)
    def _():
        drain(pr.at[pl.ds(0, 3)], p_recv)

    @pl.when(x < 3)
    def _():
        drain(pr.at[pl.ds(0, 2)], p_recv)

    for p in range(NX - 1):
        total = total + pr[p].astype(F32)
    live = lax.broadcasted_iota(jnp.int32, (COLS, LEAF), 1) < rows_ref[0]
    out_ref[...] = jnp.where(live, total, 0.0).astype(BF16)
    for finish in drains:
        finish()


def hand_over(values, leaf, values_out, leaf_out):
    leaf_out[...] = leaf[...]
    values_out[...] = values[...]


N_SEMS = 112


def body(sep_q, sep_phi, coupling, leaf_q, leaf_phi, leaf_coupling, leaf_rows):
    vmem = pl.BlockSpec(memory_space=pltpu.VMEM)
    hbm = pl.BlockSpec(memory_space=pl.ANY)
    block = (16, 128)
    scratch = [
        pltpu.VMEM((1, 328704), BF16),
        pltpu.VMEM((CROWS + 8, 128), F32),
        pltpu.VMEM((128, 1024), BF16),
        pltpu.VMEM((128, 1024), F32),
        pltpu.VMEM((LEVELS - 1, 128, 4096), BF16),
        pltpu.VMEM((1016, LEAF), BF16),
        pltpu.VMEM((1040, LEAF), BF16),
        pltpu.VMEM((512, LEAF), BF16),
        pltpu.VMEM((1024, LEAF), BF16),
        pltpu.VMEM((16, 48, 128), BF16),
        pltpu.VMEM((16, 48, 128), BF16),
        pltpu.VMEM((48, 128), BF16),
        pltpu.VMEM((8, 48, 128), BF16),
        pltpu.VMEM((14,) + block, F32),
        pltpu.VMEM((8,) + block, F32),
        pltpu.VMEM((4,) + block, F32),
        pltpu.VMEM((2,) + block, F32),
        pltpu.VMEM(block, F32),
        pltpu.VMEM((3, 128, 128), F32),
        pltpu.VMEM((16, 16, 512), BF16),
        pltpu.VMEM((8, 16, 768), BF16),
        pltpu.VMEM((4, 16, 896), BF16),
        pltpu.VMEM((2, 16, 1024), BF16),
    ]
    scratch += [pltpu.VMEM((n,) + block, BF16) for n in (16, 8, 4, 2)]
    scratch += [pltpu.VMEM(group + (NC,) + block, BF16) for group in GROUPS[:3]]
    scratch += [pltpu.VMEM((n,) + block, BF16) for n in (16, 8, 4, 2)]
    scratch += [
        pltpu.VMEM((LEVELS - 2, 128, 128), F32),
        pltpu.VMEM((COLS, LEAF), F32),
        pltpu.VMEM((NX, 4, NZ, NC) + block, BF16),
        pltpu.VMEM((NX,) + block, BF16),
        pltpu.VMEM((NX, COLS, LEAF), BF16),
        pltpu.VMEM((NX, COLS, LEAF), BF16),
        pltpu.SemaphoreType.DMA((N_SEMS,)),
    ]
    values, leaf = pl.pallas_call(
        kernel,
        out_shape=(
            jax.ShapeDtypeStruct((16 * LEVELS, COLS), BF16),
            jax.ShapeDtypeStruct((COLS, LEAF), BF16),
        ),
        in_specs=[vmem, vmem, hbm, vmem, vmem, hbm, pl.BlockSpec(memory_space=pltpu.SMEM)],
        out_specs=(vmem, vmem),
        scratch_shapes=scratch,
        compiler_params=pltpu.CompilerParams(
            collective_id=0, has_side_effects=True, vmem_limit_bytes=56 * 1024 * 1024
        ),
        cost_estimate=pl.CostEstimate(flops=2_000_000_000, bytes_accessed=4_000_000, transcendentals=0),
    )(sep_q[0].T, sep_phi[0], coupling, leaf_q[0], leaf_phi[0], leaf_coupling[0], leaf_rows)
    values, leaf = pl.pallas_call(
        hand_over,
        out_shape=(
            jax.ShapeDtypeStruct((16 * LEVELS, COLS), BF16),
            jax.ShapeDtypeStruct((COLS, LEAF), BF16),
        ),
        in_specs=[vmem, vmem],
        out_specs=(vmem, vmem),
        compiler_params=pltpu.CompilerParams(vmem_limit_bytes=56 * 1024 * 1024),
    )(values, leaf)
    return values.T[None], leaf[None]


def solution(mesh):
    in_specs = (
        P("sub", "col", None),
        P("sub", None, None),
        P("sub", None),
        P("sub", "col", None),
        P("sub", None, None),
        P("sub", "col", None),
        P("sub"),
    )
    out_specs = (P("sub", "col", None), P("sub", "col", None))
    return jax.shard_map(body, mesh=mesh, in_specs=in_specs, out_specs=out_specs, check_vma=False)
```

```python
import jax
import jax.numpy as jnp
from jax import lax
from jax.experimental import pallas as pl
from jax.experimental.pallas import tpu as pltpu
from jax.sharding import PartitionSpec as P

MESH = pl.DeviceIdType.MESH
F32 = jnp.float32
BF16 = jnp.bfloat16
NY, NZ, NC, NX = 8, 8, 2, 4
COLS = 128
LEAF = 640
GROUPS = ((8, 8), (4, 8), (2, 8), (1, 8), (1, 4), (1, 2), (1, 1))
LEVELS = len(GROUPS)
CROW = (0, 0, 256, 640, 1088, 1568, 2064)
NEAR = 3072
CL_AT = (0, 512, 1280, 2176, 3200)
CROWS = 2568


def dot_t(a, b):
    return lax.dot_general(a, b, (((0,), (0,)), ((), ())), preferred_element_type=F32)


def dot(a, b):
    return jnp.dot(a, b, preferred_element_type=F32)


def kernel(
    q_hbm, phi_hbm, c_hbm, lq_hbm, lphi_hbm, cpl_hbm, rows_ref,
    sv_ref, out_ref,
    q_ref, phi_ref, lq_ref, lphi_ref, c_flat, c_rows, spread, select, ct0, ct1, k32, kp0, kp1, cg,
    ms, mr, bs, br0, br1, br2, m3, m456, cl,
    k0, k1, kq, k3, k4, k5, k6, pv, acc,
    sems,
):
    known = (k0, k1)
    sub = lax.axis_index("sub")
    x = lax.axis_index("col")
    y, z, c = sub // 16, (sub // 2) % 8, sub % 2
    other = 1 - c
    zc = z * 2 + c
    zq = (z % 4) * 2 + c

    counter = [0]

    def new_sems(n):
        first = counter[0]
        counter[0] += n
        return [sems.at[first + i] for i in range(n)]

    def dev(y_, z_, c_):
        return ((y_ * 8 + z_) * 2 + c_, x)

    def send(src, dst, ss, rs, target):
        pltpu.make_async_remote_copy(
            src_ref=src, dst_ref=dst, send_sem=ss, recv_sem=rs,
            device_id=target, device_id_type=MESH,
        ).start()

    def drain(like, sem):
        pltpu.make_async_copy(like, like, sem).wait()

    drains = []

    fetches = []
    for src, dst, sem in zip(
        (q_hbm, phi_hbm, c_hbm, cpl_hbm, lq_hbm, lphi_hbm),
        (q_ref, phi_ref, c_flat, cg.at[x], lq_ref, lphi_ref),
        new_sems(6),
    ):
        fetches.append(pltpu.make_async_copy(src, dst, sem))
        fetches[-1].start()
    q_copy, phi_copy, c_copy, cpl_copy, lq_copy, lphi_copy = fetches

    barrier = pltpu.get_barrier_semaphore()
    for k in range(1, 16):
        d = (zc + k) % 16
        pl.semaphore_signal(barrier, inc=1, device_id=dev(y, d // 2, d % 2), device_id_type=MESH)
    half, pair = (y // 4) * 4, (y // 2) * 2
    mate = 2 * pair + 1 - y
    for k in range(1, 4):
        for i in range(NZ):
            pl.semaphore_signal(barrier, inc=1, device_id=dev(half + (y + k) % 4, i, c), device_id_type=MESH)
    for i in range(NZ):
        pl.semaphore_signal(barrier, inc=1, device_id=dev(mate, i, other), device_id_type=MESH)
    for k in range(4):
        pl.semaphore_signal(barrier, inc=1, device_id=dev(4 - half + k, z, c), device_id_type=MESH)
    for k in (1, NX - 1):
        pl.semaphore_signal(barrier, inc=1, device_id=(sub, (x + k) % NX), device_id_type=MESH)

    q_copy.wait()
    phi_copy.wait()
    phi = phi_ref[...].astype(F32)
    qf = q_ref[...].astype(F32)
    lane = lax.broadcasted_iota(jnp.int32, (8, 128), 1)
    zero = jnp.zeros((8, 128), F32)
    shared = [
        qf[32:40],
        phi[:, 3840:3968],
        qf[40:48],
        jnp.concatenate([phi[:, 3968:4064], zero[:, 0:32]], axis=1),
        qf[48:56],
        zero,
    ]
    for d in range(16):
        h, p = divmod(d, 8)
        parts = [qf[0:32]]
        for g in range(2):
            piece = jnp.zeros((8, 128), F32)
            for b in range(8 * g, min(8 * g + 8, 15)):
                block = phi[:, b * 256 + h * 128 : b * 256 + h * 128 + 128]
                shift = ((b % 8 - p) * 16) % 128
                if shift:
                    block = pltpu.roll(block, shift, 1)
                piece = jnp.where(lax.shift_right_logical(lane, 4) == b % 8, block, piece)
            parts.append(piece)
        ms[d] = jnp.concatenate(parts + shared, axis=0).astype(BF16)
    mr[zc] = ms[zc]

    pl.semaphore_wait(barrier, 15 + 24 + 8 + 4 + 2)

    base4, base5, base6 = zc - zq, zc - zc % 4, zc - c
    near4, near5, near6 = zq, zc % 4, c
    classes = (
        [8 - base4 + (near4 + i) % 8 for i in range(8)],
        [base4 + 4 - (base5 - base4) + (near5 + i) % 4 for i in range(4)],
        [base5 + 2 - (base6 - base5) + (near6 + i) % 2 for i in range(2)],
        [base6 + other],
    )

    def to_row(source, like):
        ss, rs = new_sems(4), new_sems(4)
        for n, places in enumerate(classes):
            for d in places:
                src, dst = source(n, d)
                send(src, dst, ss[n], rs[n], dev(y, d // 2, d % 2))

        def wait(sems_):
            for n, places in enumerate(classes):
                drain(like(n, len(places)), sems_[n])

        drains.append(lambda: wait(ss))
        return lambda: wait(rs)

    def factors(n, d):
        return ms.at[d, pl.ds(0, 48 + 16 * n)], mr.at[zc, pl.ds(0, 48 + 16 * n)]

    wait_factors = to_row(factors, lambda n, count: mr.at[pl.ds(0, count), pl.ds(0, 48 + 16 * n)])

    lanes = (pl.ds(0, 384), pl.ds(384, 256))
    left, right = (x + NX - 1) % NX, (x + 1) % NX
    (gr_send, gl_send, fr_send, fl_send, l0, l1, r0, r1, o_l, o_r) = new_sems(10)

    def by_core(step):
        for core in range(NC):
            @pl.when(c == core)
            def _(core=core):
                step(lanes[core], lanes[1 - core])

    def give(one, two):
        for part, rs_right in ((one, l0), (two, l1)):
            send(cpl_hbm.at[:, part], cg.at[x, :, part], gr_send, rs_right, (sub, right))
        for part, rs_left in ((two, r0), (one, r1)):
            send(cpl_hbm.at[:, part], cg.at[x, :, part], gl_send, rs_left, (sub, left))

    def pass_on(one, two):
        piece = cg.at[left, :, one]
        drain(piece, l0)
        send(piece, piece, fr_send, o_l, (sub, right))
        piece = cg.at[right, :, two]
        drain(piece, r0)
        send(piece, piece, fl_send, o_r, (sub, left))

    def wait_neighbours(one, two):
        drain(cg.at[0, :, two], l1)
        drain(cg.at[0, :, one], r1)

    def wait_opposite(one, two):
        drain(cg.at[0, :, one], o_l)
        drain(cg.at[0, :, two], o_r)

    def finish_gather(one, two):
        drain(cg.at[0], gr_send)
        drain(cg.at[0], gl_send)
        drain(cg.at[0, :, one], fr_send)
        drain(cg.at[0, :, two], fl_send)

    by_core(give)
    drains.append(lambda: by_core(finish_gather))

    c_copy.wait()
    wide_row = lax.broadcasted_iota(jnp.int32, (128, 1024), 0)
    wide_col = lax.broadcasted_iota(jnp.int32, (128, 1024), 1)
    spread[...] = jnp.where(lax.shift_right_logical(wide_col, 3) == wide_row, 1.0, 0.0).astype(BF16)
    select[...] = jnp.where((wide_col & 7) == lax.shift_right_logical(wide_row, 4), 1.0, 0.0)

    def rows_of(first, steps, each):
        def step(i, carry):
            for k in range(each):
                row = pl.multiple_of(first + (i * each + k) * 8, 8)
                at = pl.multiple_of(row * 128, 1024)
                value = c_flat[0:1, pl.ds(at, 1024)].astype(F32).reshape(8, 128)
                c_rows[pl.ds(row, 8), :] = value
            return carry

        lax.fori_loop(0, steps, step, 0)

    def arrange(s):
        rows_of(CROW[s], 4 if s == 1 else 6, 8)
        for k in range(2 if s == 1 else 3):
            block = c_rows[CROW[s] + 128 * k : CROW[s] + 128 * k + 128, :].T.astype(BF16)
            for j in range(8):
                piece = block[16 * j : 16 * j + 16]
                if k < 2:
                    ct0[s - 1, :, 256 * j + 128 * k : 256 * j + 128 * k + 128] = piece
                else:
                    ct1[s - 2, :, 128 * j : 128 * j + 128] = piece

    def dense(s, at, width):
        first = CROW[s] + NEAR // 8
        rows_of(first, *((3, 5) if s == LEVELS - 1 else (2, 8)))
        if s == LEVELS - 1:
            c_rows[CROWS : CROWS + 8, :] = jnp.zeros((8, 128), F32)
        wide = dot_t(c_rows[first : first + 128, :].astype(BF16), spread[:, 0:width]) * select[:, 0:width]
        cl[zc, :, at : at + width] = jnp.sum(wide.reshape(8, 16, width), axis=0).astype(BF16)

    for s, (at, end) in enumerate(zip(CL_AT, CL_AT[1:])):
        dense(3 + s, at, end - at)

    wait_factors()
    got = mr[:, 0:48].astype(F32)
    coords = [got[:, 8 * s : 8 * s + 8].reshape(128, 128).astype(BF16) for s in range(4)]
    shapes_lo = got[:, 32:40].reshape(128, 128).astype(BF16)
    shapes_hi = got[:, 40:48].reshape(128, 128).astype(BF16)
    bs[0:8] = dot_t(shapes_lo, coords[0]).reshape(8, 16, 128)
    (b0_send, b0_recv, b1_send, b1_recv, b2_send, b2_recv) = new_sems(6)
    br0[y] = bs[y]
    for k in range(1, NY):
        d = (y + k) % NY
        send(bs.at[d], br0.at[y], b0_send, b0_recv, dev(d, z, c))
    drains.append(lambda: drain(br0.at[pl.ds(0, 7)], b0_send))
    bs[8:12] = dot_t(shapes_hi, coords[1])[0:64].reshape(4, 16, 128)
    br1[y % 4] = bs[8 + y % 4]
    for k in range(1, 4):
        d = (y % 4 + k) % 4
        send(bs.at[8 + d], br1.at[y % 4], b1_send, b1_recv, dev((y // 4) * 4 + d, z, c))
    drains.append(lambda: drain(br1.at[pl.ds(0, 3)], b1_send))
    bs[12:14] = dot_t(shapes_hi, coords[2])[64:96].reshape(2, 16, 128)
    br2[y % 2] = bs[12 + y % 2]
    d = 1 - y % 2
    send(bs.at[12 + d], br2.at[y % 2], b2_send, b2_recv, dev((y // 2) * 2 + d, z, c))
    drains.append(lambda: drain(br2.at[0], b2_send))
    m3[...] = dot_t(shapes_hi, coords[3])[96:112]

    def lookahead(n, d):
        piece = cl.at[zc, :, pl.ds(0, CL_AT[n + 1])]
        return piece, piece

    wait_lookahead = to_row(lookahead, lambda n, count: cl.at[pl.ds(0, count), :, pl.ds(0, CL_AT[n + 1])])

    quad = mr[pl.ds(base4, 8), 48:64].astype(F32)
    two = mr[pl.ds(base5, 4), 64:80].astype(F32)
    chip = mr[pl.ds(base6, 2), 64:96].astype(F32)

    def part(block, at):
        return block[:, at : at + 8].reshape(-1, 128).astype(BF16)

    m456[0] = dot_t(part(quad, 8), part(quad, 0))
    m456[1] = dot_t(part(two, 8), part(two, 0))
    m456[2] = dot_t(part(chip, 8), part(chip, 16))
    arrange(1)

    def publish(s, modal):
        value = modal.astype(BF16)
        ny, nz = GROUPS[s]
        known[s][y % ny, z % nz, c] = value
        sv_ref[16 * s : 16 * s + 16, :] = value

    def permute(k_ref, kp):
        rows = kp.shape[0]
        each = rows // 8
        k32[0:rows] = k_ref[...].reshape(rows, 128).astype(F32)
        for j in range(8):
            kp[each * j : each * j + each] = k32[pl.ds(j, each, stride=8), :].astype(BF16)

    def spread_wide(s, during_first, during_second):
        ny, nz = GROUPS[s]
        k_ref = known[s]
        yi, zi = y % ny, z % nz
        y0, z0 = y - yi, z - zi
        (s1, r1, s2, s3, r3) = new_sems(5)
        r2 = new_sems(max(ny, nz) - 1)

        @pl.when(c == 0)
        def _():
            for k in range(1, ny):
                own = k_ref.at[yi, zi, 0]
                send(own, own, s1, r1, dev(y0 + (yi + k) % ny, z, 0))

        @pl.when(c == 1)
        def _():
            for k in range(1, nz):
                own = k_ref.at[yi, zi, 1]
                send(own, own, s1, r1, dev(y, z0 + (zi + k) % nz, 1))

        during_first()

        @pl.when(c == 0)
        def _():
            drain(k_ref.at[pl.ds(0, ny - 1), 0, 0], r1)
            own = k_ref.at[:, zi, 0]
            for k in range(1, nz):
                send(own, own, s2, r2[k - 1], dev(y, z0 + (zi + k) % nz, 0))
            send(own, own, s3, r3, dev(y, z, 1))

        @pl.when(c == 1)
        def _():
            drain(k_ref.at[0, pl.ds(0, nz - 1), 0], r1)
            own = k_ref.at[yi, :, 1]
            for k in range(1, ny):
                send(own, own, s2, r2[k - 1], dev(y0 + (yi + k) % ny, z, 1))
            send(own, own, s3, r3, dev(y, z, 0))

        during_second()

        def nearest(n):
            return sorted(range(1, n), key=lambda k: (min(k, n - k), k))

        @pl.when(c == 0)
        def _():
            for k in nearest(nz):
                piece = k_ref.at[:, (zi + nz - k) % nz, 0]
                drain(piece, r2[k - 1])
                send(piece, piece, s3, r3, dev(y, z, 1))

        @pl.when(c == 1)
        def _():
            for k in nearest(ny):
                piece = k_ref.at[(yi + ny - k) % ny, :, 1]
                drain(piece, r2[k - 1])
                send(piece, piece, s3, r3, dev(y, z, 0))

        drain(k_ref.at[:, :, 0], r3)

        def finish():
            @pl.when(c == 0)
            def _():
                drain(k_ref.at[pl.ds(0, ny - 1), 0, 0], s1)
                drain(k_ref.at[:, pl.ds(0, nz - 1), 0], s2)

            @pl.when(c == 1)
            def _():
                drain(k_ref.at[0, pl.ds(0, nz - 1), 0], s1)
                drain(k_ref.at[pl.ds(0, ny - 1), :, 0], s2)

            drain(k_ref.at[:, :, 0], s3)

        drains.append(finish)

    def spread_half(during):
        yi = y % 4
        (s0, s1, s3, r3) = new_sems(4)
        r1 = new_sems(4)
        own = k1.at[yi, z, c]
        for k in range(4):
            for i in range(1 if k == 0 else 0, NZ):
                send(own, own, s1 if k else s0, r1[k], dev(half + (y + k) % 4, (z + i) % NZ, c))
        during()
        drain(k1.at[0, pl.ds(0, 7), 0], r1[0])
        for k in (0, 1, 3, 2):
            piece = k1.at[(yi + 4 - k) % 4, :, c]
            if k:
                drain(piece, r1[k])
            send(piece, piece, s3, r3, dev(y, z, other))
        drain(k1.at[:, :, 0], r3)

        def finish():
            drain(k1.at[0, pl.ds(0, 7), 0], s0)
            drain(k1.at[pl.ds(0, 3), :, 0], s1)
            drain(k1.at[:, :, 0], s3)

        drains.append(finish)

    def spread_pair(during):
        yi = y % 2
        (s1, r1) = new_sems(2)
        own = kq.at[yi, zc, 0]

        def with_sums(n, d):
            piece = kq.at[yi, zc, pl.ds(0, 2 + n)]
            return piece, piece

        wait_row = to_row(with_sums, lambda n, count: kq.at[0, pl.ds(0, count), pl.ds(0, 2 + n)])
        for k in range(16):
            d = (zc + k) % 16
            send(own, own, s1, r1, dev(mate, d // 2, d % 2))
        during()
        wait_row()
        drain(kq.at[0, :, 0], r1)
        drains.append(lambda: drain(kq.at[0, :, 0], s1))

    def ancestors(block):
        first = k0[...].reshape(2048, 128)
        if block < 2:
            return first[1016 * block : 1016 * block + 1016]
        return jnp.concatenate([first[2032:], k1[...].reshape(1024, 128)[0:1000]], axis=0)

    drain(br0.at[pl.ds(0, 7)], b0_recv)
    publish(0, jnp.sum(br0[...], axis=0))

    def first_0():
        arrange(2)
        arrange(3)

    def second_0():
        arrange(4)
        arrange(5)
        by_core(pass_on)

    spread_wide(0, first_0, second_0)

    permute(k0, kp0)
    drain(br1.at[pl.ds(0, 3)], b1_recv)
    publish(1, jnp.sum(br1[...], axis=0) + dot(ct0[0], kp0[...]))

    def during_1():
        arrange(6)
        pv[...] = dot(ct0[1:6].reshape(80, 2048), kp0[...]).reshape(5, 16, 128)
        lq_copy.wait()
        lphi_copy.wait()
        acc[...] = dot(lq_ref[...], lphi_ref[...])

    spread_half(during_1)

    permute(k1, kp1)
    drain(br2.at[0], b2_recv)
    product = dot(ct1[...].reshape(80, 1024), kp1[...]) + pv[...].reshape(80, 128)

    def own_rows(s, at):
        return m456[s - 4, pl.ds(pl.multiple_of(at, 16), 16), :]

    blocks = (
        product[0:16] + jnp.sum(br2[...], axis=0),
        product[16:32] + m3[...],
        product[32:48] + own_rows(4, near4 * 16),
        product[48:64] + own_rows(5, near5 * 16),
        product[64:80] + own_rows(6, 64 + near6 * 16),
    )
    for n, value in enumerate(blocks):
        kq[y % 2, zc, n] = value.astype(BF16)
    sv_ref[32:48, :] = blocks[0].astype(BF16)

    def during_2():
        cpl_copy.wait()
        by_core(wait_neighbours)
        for block in range(3):
            @pl.when((block + NX - x) % NX != 2)
            def _(block=block):
                acc[...] += dot_t(ancestors(block), cg[block])

    spread_pair(during_2)

    wait_lookahead()
    above2 = kq[:, :, 0].reshape(512, 128)
    yi = y % 2
    pp3 = kq[yi, :, 1].reshape(256, 128).astype(F32)
    pp4 = kq[yi, pl.ds(base4, 8), 2].reshape(128, 128).astype(F32)
    pp5 = kq[yi, pl.ds(base5, 4), 3].reshape(64, 128).astype(F32)
    pp6 = kq[yi, pl.ds(base6, 2), 4].reshape(32, 128).astype(F32)
    c3 = cl[:, :, CL_AT[0] : CL_AT[1]].reshape(256, 512)
    c4 = cl[pl.ds(base4, 8), :, CL_AT[1] : CL_AT[2]].reshape(128, 768)
    c5 = cl[pl.ds(base5, 4), :, CL_AT[2] : CL_AT[3]].reshape(64, 896)
    c6 = cl[pl.ds(base6, 2), :, CL_AT[3] : CL_AT[4]].reshape(32, 1024)
    first = dot(jnp.concatenate([c3, c4[:, 0:512], c5[:, 0:512], c6[:, 0:512]], axis=0), above2)
    above3 = (pp3 + first[0:256]).astype(BF16)
    second = dot(jnp.concatenate([c4[:, 512:768], c5[:, 512:768], c6[:, 512:768]], axis=0), above3) + first[256:480]
    above4 = (pp4 + second[0:128]).astype(BF16)
    third = dot(jnp.concatenate([c5[:, 768:896], c6[:, 768:896]], axis=0), above4) + second[128:224]
    above5 = (pp5 + third[0:64]).astype(BF16)
    above6 = pp6 + third[64:96] + dot(c6[:, 896:960], above5)
    above6 = above6.astype(BF16)
    k3[...] = above3.reshape(16, 16, 128)
    k4[...] = above4.reshape(8, 16, 128)
    k5[...] = above5.reshape(4, 16, 128)
    k6[...] = above6.reshape(2, 16, 128)
    sv_ref[48:64, :] = k3[zc]
    sv_ref[64:80, :] = k4[near4]
    sv_ref[80:96, :] = k5[near5]
    sv_ref[96:112, :] = k6[near6]

    by_core(wait_opposite)
    for block in range(3):
        @pl.when((block + NX - x) % NX == 2)
        def _(block=block):
            acc[...] += dot_t(ancestors(block), cg[block])

    late = jnp.concatenate(
        [k1[...].reshape(1024, 128)[1000:], above2, above3, above4, above5, above6], axis=0
    )
    total = acc[...] + dot_t(late, cg[3])
    live = lax.broadcasted_iota(jnp.int32, (COLS, LEAF), 1) < rows_ref[0]
    out_ref[...] = jnp.where(live, total, 0.0).astype(BF16)
    for finish in drains:
        finish()


def hand_over(values, leaf, values_out, leaf_out):
    leaf_out[...] = leaf[...]
    values_out[...] = values[...]


N_SEMS = 112


def body(sep_q, sep_phi, coupling, leaf_q, leaf_phi, leaf_coupling, leaf_rows):
    vmem = pl.BlockSpec(memory_space=pltpu.VMEM)
    hbm = pl.BlockSpec(memory_space=pl.ANY)
    block = (16, 128)
    scratch = [
        pltpu.VMEM((56, 128), BF16),
        pltpu.VMEM((8, 4064), BF16),
        pltpu.VMEM((128, 128), BF16),
        pltpu.VMEM((128, LEAF), BF16),
        pltpu.VMEM((1, 328704), BF16),
        pltpu.VMEM((CROWS + 8, 128), F32),
        pltpu.VMEM((128, 1024), BF16),
        pltpu.VMEM((128, 1024), F32),
        pltpu.VMEM((LEVELS - 1, 16, 2048), BF16),
        pltpu.VMEM((LEVELS - 2, 16, 1024), BF16),
        pltpu.VMEM((2048, 128), F32),
        pltpu.VMEM((2048, 128), BF16),
        pltpu.VMEM((1024, 128), BF16),
        pltpu.VMEM((NX, 1016, LEAF), BF16),
        pltpu.VMEM((16, 96, 128), BF16),
        pltpu.VMEM((16, 96, 128), BF16),
        pltpu.VMEM((14,) + block, F32),
        pltpu.VMEM((8,) + block, F32),
        pltpu.VMEM((4,) + block, F32),
        pltpu.VMEM((2,) + block, F32),
        pltpu.VMEM(block, F32),
        pltpu.VMEM((3, 128, 128), F32),
        pltpu.VMEM((16, 16, CL_AT[-1]), BF16),
    ]
    scratch += [pltpu.VMEM(group + (NC,) + block, BF16) for group in GROUPS[:2]]
    scratch += [pltpu.VMEM((2, 16, 5) + block, BF16)]
    scratch += [pltpu.VMEM((n,) + block, BF16) for n in (16, 8, 4, 2)]
    scratch += [
        pltpu.VMEM((LEVELS - 2, 16, 128), F32),
        pltpu.VMEM((COLS, LEAF), F32),
        pltpu.SemaphoreType.DMA((N_SEMS,)),
    ]
    values, leaf = pl.pallas_call(
        kernel,
        out_shape=(
            jax.ShapeDtypeStruct((16 * LEVELS, COLS), BF16),
            jax.ShapeDtypeStruct((COLS, LEAF), BF16),
        ),
        in_specs=[hbm, hbm, hbm, hbm, hbm, hbm, pl.BlockSpec(memory_space=pltpu.SMEM)],
        out_specs=(vmem, vmem),
        scratch_shapes=scratch,
        compiler_params=pltpu.CompilerParams(
            collective_id=0, has_side_effects=True, vmem_limit_bytes=56 * 1024 * 1024
        ),
        cost_estimate=pl.CostEstimate(flops=2_000_000_000, bytes_accessed=4_000_000, transcendentals=0),
    )(sep_q[0].T, sep_phi[0], coupling, leaf_q[0], leaf_phi[0], leaf_coupling[0], leaf_rows)
    values, leaf = pl.pallas_call(
        hand_over,
        out_shape=(
            jax.ShapeDtypeStruct((16 * LEVELS, COLS), BF16),
            jax.ShapeDtypeStruct((COLS, LEAF), BF16),
        ),
        in_specs=[vmem, vmem],
        out_specs=(vmem, vmem),
        compiler_params=pltpu.CompilerParams(vmem_limit_bytes=56 * 1024 * 1024),
    )(values, leaf)
    return values.T[None], leaf[None]


def solution(mesh):
    in_specs = (
        P("sub", "col", None),
        P("sub", None, None),
        P("sub", None),
        P("sub", "col", None),
        P("sub", None, None),
        P("sub", "col", None),
        P("sub"),
    )
    out_specs = (P("sub", "col", None), P("sub", "col", None))
    return jax.shard_map(body, mesh=mesh, in_specs=in_specs, out_specs=out_specs, check_vma=False)
```

```python
import jax
import jax.numpy as jnp
from jax import lax
from jax.experimental import pallas as pl
from jax.experimental.pallas import tpu as pltpu
from jax.sharding import PartitionSpec as P

MESH = pl.DeviceIdType.MESH
F32 = jnp.float32
BF16 = jnp.bfloat16
NY, NZ, NC, NX = 8, 8, 2, 4
COLS = 128
LEAF = 640
GROUPS = ((8, 8), (4, 8), (2, 8), (1, 8), (1, 4), (1, 2), (1, 1))
LEVELS = len(GROUPS)
CROW = (0, 0, 256, 640, 1088, 1568, 2064)
NEAR = 3072
CL_AT = (0, 512, 1280, 2176, 3200)
CROWS = 2568


def dot_t(a, b):
    return lax.dot_general(a, b, (((0,), (0,)), ((), ())), preferred_element_type=F32)


def dot(a, b):
    return jnp.dot(a, b, preferred_element_type=F32)


def kernel(
    q_hbm, phi_hbm, c_hbm, lq_hbm, lphi_hbm, cpl_hbm, rows_ref,
    sv_ref, out_ref,
    q_ref, phi_ref, lq_ref, lphi_ref, c_flat, c_rows, spread, select, ct0, ct1, k32, kp0, kp1, cg,
    ms, mr, bs, br0, br1, br2, m3, m456, cl,
    k0, k1, kq, k3, k4, k5, k6, pv, acc,
    sems,
):
    known = (k0, k1)
    sub = lax.axis_index("sub")
    x = lax.axis_index("col")
    y, z, c = sub // 16, (sub // 2) % 8, sub % 2
    other = 1 - c
    zc = z * 2 + c
    zq = (z % 4) * 2 + c

    counter = [0]

    def new_sems(n):
        first = counter[0]
        counter[0] += n
        return [sems.at[first + i] for i in range(n)]

    def dev(y_, z_, c_):
        return ((y_ * 8 + z_) * 2 + c_, x)

    def send(src, dst, ss, rs, target):
        pltpu.make_async_remote_copy(
            src_ref=src, dst_ref=dst, send_sem=ss, recv_sem=rs,
            device_id=target, device_id_type=MESH,
        ).start()

    def drain(like, sem):
        pltpu.make_async_copy(like, like, sem).wait()

    drains = []

    fetches = []
    for src, dst, sem in zip(
        (q_hbm, phi_hbm, c_hbm, cpl_hbm, lq_hbm, lphi_hbm),
        (q_ref, phi_ref, c_flat, cg.at[x], lq_ref, lphi_ref),
        new_sems(6),
    ):
        fetches.append(pltpu.make_async_copy(src, dst, sem))
    q_copy, phi_copy, c_copy, cpl_copy, lq_copy, lphi_copy = fetches
    q_copy.start()
    phi_copy.start()

    barrier = pltpu.get_barrier_semaphore()
    for k in range(1, 16):
        d = (zc + k) % 16
        pl.semaphore_signal(barrier, inc=1, device_id=dev(y, d // 2, d % 2), device_id_type=MESH)
    half, pair = (y // 4) * 4, (y // 2) * 2
    mate = 2 * pair + 1 - y
    for k in range(1, 4):
        for i in range(NZ):
            pl.semaphore_signal(barrier, inc=1, device_id=dev(half + (y + k) % 4, i, c), device_id_type=MESH)
    for i in range(NZ):
        pl.semaphore_signal(barrier, inc=1, device_id=dev(mate, i, other), device_id_type=MESH)
    for k in range(4):
        pl.semaphore_signal(barrier, inc=1, device_id=dev(4 - half + k, z, c), device_id_type=MESH)
    for k in (1, NX - 1):
        pl.semaphore_signal(barrier, inc=1, device_id=(sub, (x + k) % NX), device_id_type=MESH)

    for fetch in (c_copy, cpl_copy, lq_copy, lphi_copy):
        fetch.start()

    q_copy.wait()
    phi_copy.wait()
    phi = phi_ref[...].astype(F32)
    qf = q_ref[...].astype(F32)
    lane = lax.broadcasted_iota(jnp.int32, (8, 128), 1)
    zero = jnp.zeros((8, 128), F32)
    shared = [
        qf[32:40],
        phi[:, 3840:3968],
        qf[40:48],
        jnp.concatenate([phi[:, 3968:4064], zero[:, 0:32]], axis=1),
        qf[48:56],
        zero,
    ]
    for d in range(16):
        h, p = divmod(d, 8)
        parts = [qf[0:32]]
        for g in range(2):
            piece = jnp.zeros((8, 128), F32)
            for b in range(8 * g, min(8 * g + 8, 15)):
                block = phi[:, b * 256 + h * 128 : b * 256 + h * 128 + 128]
                shift = ((b % 8 - p) * 16) % 128
                if shift:
                    block = pltpu.roll(block, shift, 1)
                piece = jnp.where(lax.shift_right_logical(lane, 4) == b % 8, block, piece)
            parts.append(piece)
        ms[d] = jnp.concatenate(parts + shared, axis=0).astype(BF16)
    mr[zc] = ms[zc]

    pl.semaphore_wait(barrier, 15 + 24 + 8 + 4 + 2)

    lanes = (pl.ds(0, 384), pl.ds(384, 256))
    left, right = (x + NX - 1) % NX, (x + 1) % NX
    (gr_send, gl_send, fr_send, fl_send, l0, l1, r0, r1, o_l, o_r) = new_sems(10)

    def by_core(step):
        for core in range(NC):
            @pl.when(c == core)
            def _(core=core):
                step(lanes[core], lanes[1 - core])

    def give(one, two):
        for part, rs_right in ((one, l0), (two, l1)):
            send(cpl_hbm.at[:, part], cg.at[x, :, part], gr_send, rs_right, (sub, right))
        for part, rs_left in ((two, r0), (one, r1)):
            send(cpl_hbm.at[:, part], cg.at[x, :, part], gl_send, rs_left, (sub, left))

    def pass_on(one, two):
        piece = cg.at[left, :, one]
        drain(piece, l0)
        send(piece, piece, fr_send, o_l, (sub, right))
        piece = cg.at[right, :, two]
        drain(piece, r0)
        send(piece, piece, fl_send, o_r, (sub, left))

    def wait_neighbours(one, two):
        drain(cg.at[0, :, two], l1)
        drain(cg.at[0, :, one], r1)

    def wait_opposite(one, two):
        drain(cg.at[0, :, one], o_l)
        drain(cg.at[0, :, two], o_r)

    def finish_gather(one, two):
        drain(cg.at[0], gr_send)
        drain(cg.at[0], gl_send)
        drain(cg.at[0, :, one], fr_send)
        drain(cg.at[0, :, two], fl_send)

    by_core(give)

    base4, base5, base6 = zc - zq, zc - zc % 4, zc - c
    near4, near5, near6 = zq, zc % 4, c
    classes = (
        [8 - base4 + (near4 + i) % 8 for i in range(8)],
        [base4 + 4 - (base5 - base4) + (near5 + i) % 4 for i in range(4)],
        [base5 + 2 - (base6 - base5) + (near6 + i) % 2 for i in range(2)],
        [base6 + other],
    )

    def to_row(source, like):
        ss, rs = new_sems(4), new_sems(4)
        for n, places in enumerate(classes):
            for d in places:
                src, dst = source(n, d)
                send(src, dst, ss[n], rs[n], dev(y, d // 2, d % 2))

        def wait(sems_):
            for n, places in enumerate(classes):
                drain(like(n, len(places)), sems_[n])

        drains.append(lambda: wait(ss))
        return lambda: wait(rs)

    def factors(n, d):
        return ms.at[d, pl.ds(0, 48 + 16 * n)], mr.at[zc, pl.ds(0, 48 + 16 * n)]

    wait_factors = to_row(factors, lambda n, count: mr.at[pl.ds(0, count), pl.ds(0, 48 + 16 * n)])

    c_copy.wait()
    wide_row = lax.broadcasted_iota(jnp.int32, (128, 1024), 0)
    wide_col = lax.broadcasted_iota(jnp.int32, (128, 1024), 1)
    spread[...] = jnp.where(lax.shift_right_logical(wide_col, 3) == wide_row, 1.0, 0.0).astype(BF16)
    select[...] = jnp.where((wide_col & 7) == lax.shift_right_logical(wide_row, 4), 1.0, 0.0)

    def rows_of(first, steps, each):
        def step(i, carry):
            for k in range(each):
                row = pl.multiple_of(first + (i * each + k) * 8, 8)
                at = pl.multiple_of(row * 128, 1024)
                value = c_flat[0:1, pl.ds(at, 1024)].astype(F32).reshape(8, 128)
                c_rows[pl.ds(row, 8), :] = value
            return carry

        lax.fori_loop(0, steps, step, 0)

    def arrange(s):
        rows_of(CROW[s], 4 if s == 1 else 6, 8)
        for k in range(2 if s == 1 else 3):
            block = c_rows[CROW[s] + 128 * k : CROW[s] + 128 * k + 128, :].T.astype(BF16)
            for j in range(8):
                piece = block[16 * j : 16 * j + 16]
                if k < 2:
                    ct0[s - 1, :, 256 * j + 128 * k : 256 * j + 128 * k + 128] = piece
                else:
                    ct1[s - 2, :, 128 * j : 128 * j + 128] = piece

    def dense(s, at, width):
        first = CROW[s] + NEAR // 8
        rows_of(first, *((3, 5) if s == LEVELS - 1 else (2, 8)))
        if s == LEVELS - 1:
            c_rows[CROWS : CROWS + 8, :] = jnp.zeros((8, 128), F32)
        wide = dot_t(c_rows[first : first + 128, :].astype(BF16), spread[:, 0:width]) * select[:, 0:width]
        cl[zc, :, at : at + width] = jnp.sum(wide.reshape(8, 16, width), axis=0).astype(BF16)

    for s, (at, end) in enumerate(zip(CL_AT, CL_AT[1:])):
        dense(3 + s, at, end - at)

    wait_factors()
    got = mr[:, 0:48].astype(F32)
    coords = [got[:, 8 * s : 8 * s + 8].reshape(128, 128).astype(BF16) for s in range(4)]
    shapes_lo = got[:, 32:40].reshape(128, 128).astype(BF16)
    shapes_hi = got[:, 40:48].reshape(128, 128).astype(BF16)
    bs[0:8] = dot_t(shapes_lo, coords[0]).reshape(8, 16, 128)
    (b0_send, b0_recv, b1_send, b1_recv, b2_send, b2_recv) = new_sems(6)
    br0[y] = bs[y]
    for k in range(1, NY):
        d = (y + k) % NY
        send(bs.at[d], br0.at[y], b0_send, b0_recv, dev(d, z, c))
    drains.append(lambda: drain(br0.at[pl.ds(0, 7)], b0_send))
    bs[8:12] = dot_t(shapes_hi, coords[1])[0:64].reshape(4, 16, 128)
    br1[y % 4] = bs[8 + y % 4]
    for k in range(1, 4):
        d = (y % 4 + k) % 4
        send(bs.at[8 + d], br1.at[y % 4], b1_send, b1_recv, dev((y // 4) * 4 + d, z, c))
    drains.append(lambda: drain(br1.at[pl.ds(0, 3)], b1_send))
    bs[12:14] = dot_t(shapes_hi, coords[2])[64:96].reshape(2, 16, 128)
    br2[y % 2] = bs[12 + y % 2]
    d = 1 - y % 2
    send(bs.at[12 + d], br2.at[y % 2], b2_send, b2_recv, dev((y // 2) * 2 + d, z, c))
    drains.append(lambda: drain(br2.at[0], b2_send))
    m3[...] = dot_t(shapes_hi, coords[3])[96:112]

    def lookahead(n, d):
        piece = cl.at[zc, :, pl.ds(0, CL_AT[n + 1])]
        return piece, piece

    wait_lookahead = to_row(lookahead, lambda n, count: cl.at[pl.ds(0, count), :, pl.ds(0, CL_AT[n + 1])])

    quad = mr[pl.ds(base4, 8), 48:64].astype(F32)
    two = mr[pl.ds(base5, 4), 64:80].astype(F32)
    chip = mr[pl.ds(base6, 2), 64:96].astype(F32)

    def part(block, at):
        return block[:, at : at + 8].reshape(-1, 128).astype(BF16)

    m456[0] = dot_t(part(quad, 8), part(quad, 0))
    m456[1] = dot_t(part(two, 8), part(two, 0))
    m456[2] = dot_t(part(chip, 8), part(chip, 16))
    arrange(1)

    def publish(s, modal):
        value = modal.astype(BF16)
        ny, nz = GROUPS[s]
        known[s][y % ny, z % nz, c] = value
        sv_ref[16 * s : 16 * s + 16, :] = value

    def permute(k_ref, kp):
        rows = kp.shape[0]
        each = rows // 8
        k32[0:rows] = k_ref[...].reshape(rows, 128).astype(F32)
        for j in range(8):
            kp[each * j : each * j + each] = k32[pl.ds(j, each, stride=8), :].astype(BF16)

    def spread_wide(s, during_first, during_second):
        ny, nz = GROUPS[s]
        k_ref = known[s]
        yi, zi = y % ny, z % nz
        y0, z0 = y - yi, z - zi
        (s1, r1, s2, s3, r3) = new_sems(5)
        r2 = new_sems(max(ny, nz) - 1)

        @pl.when(c == 0)
        def _():
            for k in range(1, ny):
                own = k_ref.at[yi, zi, 0]
                send(own, own, s1, r1, dev(y0 + (yi + k) % ny, z, 0))

        @pl.when(c == 1)
        def _():
            for k in range(1, nz):
                own = k_ref.at[yi, zi, 1]
                send(own, own, s1, r1, dev(y, z0 + (zi + k) % nz, 1))

        during_first()

        @pl.when(c == 0)
        def _():
            drain(k_ref.at[pl.ds(0, ny - 1), 0, 0], r1)
            own = k_ref.at[:, zi, 0]
            for k in range(1, nz):
                send(own, own, s2, r2[k - 1], dev(y, z0 + (zi + k) % nz, 0))
            send(own, own, s3, r3, dev(y, z, 1))

        @pl.when(c == 1)
        def _():
            drain(k_ref.at[0, pl.ds(0, nz - 1), 0], r1)
            own = k_ref.at[yi, :, 1]
            for k in range(1, ny):
                send(own, own, s2, r2[k - 1], dev(y0 + (yi + k) % ny, z, 1))
            send(own, own, s3, r3, dev(y, z, 0))

        during_second()

        def nearest(n):
            return sorted(range(1, n), key=lambda k: (min(k, n - k), k))

        @pl.when(c == 0)
        def _():
            for k in nearest(nz):
                piece = k_ref.at[:, (zi + nz - k) % nz, 0]
                drain(piece, r2[k - 1])
                send(piece, piece, s3, r3, dev(y, z, 1))

        @pl.when(c == 1)
        def _():
            for k in nearest(ny):
                piece = k_ref.at[(yi + ny - k) % ny, :, 1]
                drain(piece, r2[k - 1])
                send(piece, piece, s3, r3, dev(y, z, 0))

        drain(k_ref.at[:, :, 0], r3)

        def finish():
            @pl.when(c == 0)
            def _():
                drain(k_ref.at[pl.ds(0, ny - 1), 0, 0], s1)
                drain(k_ref.at[:, pl.ds(0, nz - 1), 0], s2)

            @pl.when(c == 1)
            def _():
                drain(k_ref.at[0, pl.ds(0, nz - 1), 0], s1)
                drain(k_ref.at[pl.ds(0, ny - 1), :, 0], s2)

            drain(k_ref.at[:, :, 0], s3)

        drains.append(finish)

    def spread_half(during):
        yi = y % 4
        (s0, s1, s3, r3) = new_sems(4)
        r1 = new_sems(4)
        own = k1.at[yi, z, c]
        for k in range(4):
            for i in range(1 if k == 0 else 0, NZ):
                send(own, own, s1 if k else s0, r1[k], dev(half + (y + k) % 4, (z + i) % NZ, c))
        during()
        drain(k1.at[0, pl.ds(0, 7), 0], r1[0])
        for k in (0, 1, 3, 2):
            piece = k1.at[(yi + 4 - k) % 4, :, c]
            if k:
                drain(piece, r1[k])
            send(piece, piece, s3, r3, dev(y, z, other))
        drain(k1.at[:, :, 0], r3)

        def finish():
            drain(k1.at[0, pl.ds(0, 7), 0], s0)
            drain(k1.at[pl.ds(0, 3), :, 0], s1)
            drain(k1.at[:, :, 0], s3)

        drains.append(finish)

    def spread_pair(during):
        yi = y % 2
        (s1, r1) = new_sems(2)
        own = kq.at[yi, zc, 0]

        def with_sums(n, d):
            piece = kq.at[yi, zc, pl.ds(0, 2 + n)]
            return piece, piece

        wait_row = to_row(with_sums, lambda n, count: kq.at[0, pl.ds(0, count), pl.ds(0, 2 + n)])
        for k in range(16):
            d = (zc + k) % 16
            send(own, own, s1, r1, dev(mate, d // 2, d % 2))
        during()
        wait_row()
        drain(kq.at[0, :, 0], r1)
        drains.append(lambda: drain(kq.at[0, :, 0], s1))

    def ancestors(block):
        first = k0[...].reshape(2048, 128)
        if block < 2:
            return first[1016 * block : 1016 * block + 1016]
        return jnp.concatenate([first[2032:], k1[...].reshape(1024, 128)[0:1000]], axis=0)

    drain(br0.at[pl.ds(0, 7)], b0_recv)
    publish(0, jnp.sum(br0[...], axis=0))

    def first_0():
        arrange(2)
        arrange(3)

    def second_0():
        arrange(4)
        arrange(5)
        by_core(pass_on)

    spread_wide(0, first_0, second_0)

    permute(k0, kp0)
    drain(br1.at[pl.ds(0, 3)], b1_recv)
    publish(1, jnp.sum(br1[...], axis=0) + dot(ct0[0], kp0[...]))

    def during_1():
        arrange(6)
        pv[...] = dot(ct0[1:6].reshape(80, 2048), kp0[...]).reshape(5, 16, 128)
        lq_copy.wait()
        lphi_copy.wait()
        acc[...] = dot(lq_ref[...], lphi_ref[...])

    spread_half(during_1)

    permute(k1, kp1)
    drain(br2.at[0], b2_recv)
    product = dot(ct1[...].reshape(80, 1024), kp1[...]) + pv[...].reshape(80, 128)

    def flush(keep):
        while len(drains) > keep:
            drains.pop(0)()

    def own_rows(s, at):
        return m456[s - 4, pl.ds(pl.multiple_of(at, 16), 16), :]

    blocks = (
        product[0:16] + jnp.sum(br2[...], axis=0),
        product[16:32] + m3[...],
        product[32:48] + own_rows(4, near4 * 16),
        product[48:64] + own_rows(5, near5 * 16),
        product[64:80] + own_rows(6, 64 + near6 * 16),
    )
    for n, value in enumerate(blocks):
        kq[y % 2, zc, n] = value.astype(BF16)
    sv_ref[32:48, :] = blocks[0].astype(BF16)

    def during_2():
        cpl_copy.wait()
        by_core(wait_neighbours)
        for block in range(3):
            @pl.when((block + NX - x) % NX != 2)
            def _(block=block):
                acc[...] += dot_t(ancestors(block), cg[block])

        flush(1)

    spread_pair(during_2)

    wait_lookahead()
    above2 = kq[:, :, 0].reshape(512, 128)
    yi = y % 2
    pp3 = kq[yi, :, 1].reshape(256, 128).astype(F32)
    pp4 = kq[yi, pl.ds(base4, 8), 2].reshape(128, 128).astype(F32)
    pp5 = kq[yi, pl.ds(base5, 4), 3].reshape(64, 128).astype(F32)
    pp6 = kq[yi, pl.ds(base6, 2), 4].reshape(32, 128).astype(F32)
    c3 = cl[:, :, CL_AT[0] : CL_AT[1]].reshape(256, 512)
    c4 = cl[pl.ds(base4, 8), :, CL_AT[1] : CL_AT[2]].reshape(128, 768)
    c5 = cl[pl.ds(base5, 4), :, CL_AT[2] : CL_AT[3]].reshape(64, 896)
    c6 = cl[pl.ds(base6, 2), :, CL_AT[3] : CL_AT[4]].reshape(32, 1024)
    first = dot(jnp.concatenate([c3, c4[:, 0:512], c5[:, 0:512], c6[:, 0:512]], axis=0), above2)
    above3 = (pp3 + first[0:256]).astype(BF16)
    second = dot(jnp.concatenate([c4[:, 512:768], c5[:, 512:768], c6[:, 512:768]], axis=0), above3) + first[256:480]
    above4 = (pp4 + second[0:128]).astype(BF16)
    third = dot(jnp.concatenate([c5[:, 768:896], c6[:, 768:896]], axis=0), above4) + second[128:224]
    above5 = (pp5 + third[0:64]).astype(BF16)
    above6 = pp6 + third[64:96] + dot(c6[:, 896:960], above5)
    above6 = above6.astype(BF16)
    k3[...] = above3.reshape(16, 16, 128)
    k4[...] = above4.reshape(8, 16, 128)
    k5[...] = above5.reshape(4, 16, 128)
    k6[...] = above6.reshape(2, 16, 128)
    sv_ref[48:64, :] = k3[zc]
    sv_ref[64:80, :] = k4[near4]
    sv_ref[80:96, :] = k5[near5]
    sv_ref[96:112, :] = k6[near6]

    late = jnp.concatenate(
        [k1[...].reshape(1024, 128)[1000:], above2, above3, above4, above5, above6], axis=0
    )

    @pl.when(x != 1)
    def _():
        acc[...] += dot_t(late, cg[3])

    flush(0)
    by_core(wait_opposite)
    by_core(finish_gather)
    for block in range(NX):
        @pl.when((block + NX - x) % NX == 2)
        def _(block=block):
            acc[...] += dot_t(late if block == 3 else ancestors(block), cg[block])

    total = acc[...]
    live = lax.broadcasted_iota(jnp.int32, (COLS, LEAF), 1) < rows_ref[0]
    out_ref[...] = jnp.where(live, total, 0.0).astype(BF16)


def hand_over(values, leaf, values_out, leaf_out):
    leaf_out[...] = leaf[...]
    values_out[...] = values[...]


N_SEMS = 112


def body(sep_q, sep_phi, coupling, leaf_q, leaf_phi, leaf_coupling, leaf_rows):
    vmem = pl.BlockSpec(memory_space=pltpu.VMEM)
    hbm = pl.BlockSpec(memory_space=pl.ANY)
    block = (16, 128)
    scratch = [
        pltpu.VMEM((56, 128), BF16),
        pltpu.VMEM((8, 4064), BF16),
        pltpu.VMEM((128, 128), BF16),
        pltpu.VMEM((128, LEAF), BF16),
        pltpu.VMEM((1, 328704), BF16),
        pltpu.VMEM((CROWS + 8, 128), F32),
        pltpu.VMEM((128, 1024), BF16),
        pltpu.VMEM((128, 1024), F32),
        pltpu.VMEM((LEVELS - 1, 16, 2048), BF16),
        pltpu.VMEM((LEVELS - 2, 16, 1024), BF16),
        pltpu.VMEM((2048, 128), F32),
        pltpu.VMEM((2048, 128), BF16),
        pltpu.VMEM((1024, 128), BF16),
        pltpu.VMEM((NX, 1016, LEAF), BF16),
        pltpu.VMEM((16, 96, 128), BF16),
        pltpu.VMEM((16, 96, 128), BF16),
        pltpu.VMEM((14,) + block, F32),
        pltpu.VMEM((8,) + block, F32),
        pltpu.VMEM((4,) + block, F32),
        pltpu.VMEM((2,) + block, F32),
        pltpu.VMEM(block, F32),
        pltpu.VMEM((3, 128, 128), F32),
        pltpu.VMEM((16, 16, CL_AT[-1]), BF16),
    ]
    scratch += [pltpu.VMEM(group + (NC,) + block, BF16) for group in GROUPS[:2]]
    scratch += [pltpu.VMEM((2, 16, 5) + block, BF16)]
    scratch += [pltpu.VMEM((n,) + block, BF16) for n in (16, 8, 4, 2)]
    scratch += [
        pltpu.VMEM((LEVELS - 2, 16, 128), F32),
        pltpu.VMEM((COLS, LEAF), F32),
        pltpu.SemaphoreType.DMA((N_SEMS,)),
    ]
    values, leaf = pl.pallas_call(
        kernel,
        out_shape=(
            jax.ShapeDtypeStruct((16 * LEVELS, COLS), BF16),
            jax.ShapeDtypeStruct((COLS, LEAF), BF16),
        ),
        in_specs=[hbm, hbm, hbm, hbm, hbm, hbm, pl.BlockSpec(memory_space=pltpu.SMEM)],
        out_specs=(vmem, vmem),
        scratch_shapes=scratch,
        compiler_params=pltpu.CompilerParams(
            collective_id=0, has_side_effects=True, vmem_limit_bytes=56 * 1024 * 1024
        ),
        cost_estimate=pl.CostEstimate(flops=2_000_000_000, bytes_accessed=4_000_000, transcendentals=0),
    )(sep_q[0].T, sep_phi[0], coupling, leaf_q[0], leaf_phi[0], leaf_coupling[0], leaf_rows)
    values, leaf = pl.pallas_call(
        hand_over,
        out_shape=(
            jax.ShapeDtypeStruct((16 * LEVELS, COLS), BF16),
            jax.ShapeDtypeStruct((COLS, LEAF), BF16),
        ),
        in_specs=[vmem, vmem],
        out_specs=(vmem, vmem),
        compiler_params=pltpu.CompilerParams(vmem_limit_bytes=56 * 1024 * 1024),
    )(values, leaf)
    return values.T[None], leaf[None]


def solution(mesh):
    in_specs = (
        P("sub", "col", None),
        P("sub", None, None),
        P("sub", None),
        P("sub", "col", None),
        P("sub", None, None),
        P("sub", "col", None),
        P("sub"),
    )
    out_specs = (P("sub", "col", None), P("sub", "col", None))
    return jax.shard_map(body, mesh=mesh, in_specs=in_specs, out_specs=out_specs, check_vma=False)
```

```python
import jax
import jax.numpy as jnp
from jax import lax
from jax.experimental import pallas as pl
from jax.experimental.pallas import tpu as pltpu
from jax.sharding import PartitionSpec as P

MESH = pl.DeviceIdType.MESH
F32 = jnp.float32
BF16 = jnp.bfloat16
NY, NZ, NC, NX = 8, 8, 2, 4
COLS = 128
LEAF = 640
GROUPS = ((8, 8), (4, 8), (2, 8), (1, 8), (1, 4), (1, 2), (1, 1))
LEVELS = len(GROUPS)
CROW = (0, 0, 256, 640, 1088, 1568, 2064)
NEAR = 3072
CL_AT = (0, 512, 1280, 2176, 3200)
CROWS = 2568


def dot_t(a, b):
    return lax.dot_general(a, b, (((0,), (0,)), ((), ())), preferred_element_type=F32)


def dot(a, b):
    return jnp.dot(a, b, preferred_element_type=F32)


def kernel(
    q_hbm, phi_hbm, c_hbm, lq_hbm, lphi_hbm, cpl_hbm, rows_ref,
    sv_ref, out_ref,
    q_ref, phi_ref, lq_ref, lphi_ref, c_flat, c_rows, spread, select, ct0, ct1, k32, kp0, kp1, cg,
    ms, mr, bs, br0, br1, br2, m3, m456, cl,
    k0, k1, kq, k3, k4, k5, k6, pv, acc,
    sems,
):
    known = (k0, k1)
    sub = lax.axis_index("sub")
    x = lax.axis_index("col")
    y, z, c = sub // 16, (sub // 2) % 8, sub % 2
    other = 1 - c
    zc = z * 2 + c
    zq = (z % 4) * 2 + c

    counter = [0]

    def new_sems(n):
        first = counter[0]
        counter[0] += n
        return [sems.at[first + i] for i in range(n)]

    def dev(y_, z_, c_):
        return ((y_ * 8 + z_) * 2 + c_, x)

    def send(src, dst, ss, rs, target):
        pltpu.make_async_remote_copy(
            src_ref=src, dst_ref=dst, send_sem=ss, recv_sem=rs,
            device_id=target, device_id_type=MESH,
        ).start()

    def drain(like, sem):
        pltpu.make_async_copy(like, like, sem).wait()

    drains = []

    fetches = []
    for src, dst, sem in zip(
        (q_hbm, phi_hbm, c_hbm, cpl_hbm, lq_hbm, lphi_hbm),
        (q_ref, phi_ref, c_flat, cg.at[x], lq_ref, lphi_ref),
        new_sems(6),
    ):
        fetches.append(pltpu.make_async_copy(src, dst, sem))
    q_copy, phi_copy, c_copy, cpl_copy, lq_copy, lphi_copy = fetches
    q_copy.start()
    phi_copy.start()

    barrier = pltpu.get_barrier_semaphore()
    for k in range(1, 16):
        d = (zc + k) % 16
        pl.semaphore_signal(barrier, inc=1, device_id=dev(y, d // 2, d % 2), device_id_type=MESH)
    half, pair = (y // 4) * 4, (y // 2) * 2
    mate = 2 * pair + 1 - y
    for k in range(1, 4):
        for i in range(NZ):
            pl.semaphore_signal(barrier, inc=1, device_id=dev(half + (y + k) % 4, i, c), device_id_type=MESH)
    for i in range(NZ):
        pl.semaphore_signal(barrier, inc=1, device_id=dev(mate, i, other), device_id_type=MESH)
    for k in range(4):
        pl.semaphore_signal(barrier, inc=1, device_id=dev(4 - half + k, z, c), device_id_type=MESH)
    for k in (1, NX - 1):
        pl.semaphore_signal(barrier, inc=1, device_id=(sub, (x + k) % NX), device_id_type=MESH)

    for fetch in (c_copy, cpl_copy, lq_copy, lphi_copy):
        fetch.start()

    q_copy.wait()
    phi_copy.wait()
    phi = phi_ref[...].astype(F32)
    qf = q_ref[...].astype(F32)
    lane = lax.broadcasted_iota(jnp.int32, (8, 128), 1)
    zero = jnp.zeros((8, 128), F32)
    shared = [
        qf[32:40],
        phi[:, 3840:3968],
        qf[40:48],
        jnp.concatenate([phi[:, 3968:4064], zero[:, 0:32]], axis=1),
        qf[48:56],
        zero,
    ]
    for d in range(16):
        h, p = divmod(d, 8)
        parts = [qf[0:32]]
        for g in range(2):
            piece = jnp.zeros((8, 128), F32)
            for b in range(8 * g, min(8 * g + 8, 15)):
                block = phi[:, b * 256 + h * 128 : b * 256 + h * 128 + 128]
                shift = ((b % 8 - p) * 16) % 128
                if shift:
                    block = pltpu.roll(block, shift, 1)
                piece = jnp.where(lax.shift_right_logical(lane, 4) == b % 8, block, piece)
            parts.append(piece)
        ms[d] = jnp.concatenate(parts + shared, axis=0).astype(BF16)
    mr[zc] = ms[zc]

    pl.semaphore_wait(barrier, 15 + 24 + 8 + 4 + 2)

    lanes = (pl.ds(0, 384), pl.ds(384, 256))
    left, right = (x + NX - 1) % NX, (x + 1) % NX
    (gr_send, gl_send, fr_send, fl_send, l0, l1, r0, r1, o_l, o_r) = new_sems(10)

    def by_core(step):
        for core in range(NC):
            @pl.when(c == core)
            def _(core=core):
                step(lanes[core], lanes[1 - core])

    def give(one, two):
        for part, rs_right in ((one, l0), (two, l1)):
            send(cpl_hbm.at[:, part], cg.at[x, :, part], gr_send, rs_right, (sub, right))
        for part, rs_left in ((two, r0), (one, r1)):
            send(cpl_hbm.at[:, part], cg.at[x, :, part], gl_send, rs_left, (sub, left))

    def pass_on(one, two):
        piece = cg.at[left, :, one]
        drain(piece, l0)
        send(piece, piece, fr_send, o_l, (sub, right))
        piece = cg.at[right, :, two]
        drain(piece, r0)
        send(piece, piece, fl_send, o_r, (sub, left))

    def wait_neighbours(one, two):
        drain(cg.at[0, :, two], l1)
        drain(cg.at[0, :, one], r1)

    def wait_opposite(one, two):
        drain(cg.at[0, :, one], o_l)
        drain(cg.at[0, :, two], o_r)

    def finish_gather(one, two):
        drain(cg.at[0], gr_send)
        drain(cg.at[0], gl_send)
        drain(cg.at[0, :, one], fr_send)
        drain(cg.at[0, :, two], fl_send)

    by_core(give)

    base4, base5, base6 = zc - zq, zc - zc % 4, zc - c
    near4, near5, near6 = zq, zc % 4, c
    classes = (
        [8 - base4 + (near4 + i) % 8 for i in range(8)],
        [base4 + 4 - (base5 - base4) + (near5 + i) % 4 for i in range(4)],
        [base5 + 2 - (base6 - base5) + (near6 + i) % 2 for i in range(2)],
        [base6 + other],
    )

    def to_row(source, like):
        ss, rs = new_sems(4), new_sems(4)
        for n, places in enumerate(classes):
            for d in places:
                src, dst = source(n, d)
                send(src, dst, ss[n], rs[n], dev(y, d // 2, d % 2))

        def wait(sems_):
            for n, places in enumerate(classes):
                drain(like(n, len(places)), sems_[n])

        drains.append(lambda: wait(ss))
        return lambda: wait(rs)

    def factors(n, d):
        return ms.at[d, pl.ds(0, 48 + 16 * n)], mr.at[zc, pl.ds(0, 48 + 16 * n)]

    wait_factors = to_row(factors, lambda n, count: mr.at[pl.ds(0, count), pl.ds(0, 48 + 16 * n)])

    c_copy.wait()
    wide_row = lax.broadcasted_iota(jnp.int32, (128, 1024), 0)
    wide_col = lax.broadcasted_iota(jnp.int32, (128, 1024), 1)
    spread[...] = jnp.where(lax.shift_right_logical(wide_col, 3) == wide_row, 1.0, 0.0).astype(BF16)
    select[...] = jnp.where((wide_col & 7) == lax.shift_right_logical(wide_row, 4), 1.0, 0.0)

    def rows_of(first, steps, each):
        def step(i, carry):
            for k in range(each):
                row = pl.multiple_of(first + (i * each + k) * 8, 8)
                at = pl.multiple_of(row * 128, 1024)
                value = c_flat[0:1, pl.ds(at, 1024)].astype(F32).reshape(8, 128)
                c_rows[pl.ds(row, 8), :] = value
            return carry

        lax.fori_loop(0, steps, step, 0)

    def arrange(s):
        rows_of(CROW[s], 4 if s == 1 else 6, 8)
        for k in range(2 if s == 1 else 3):
            block = c_rows[CROW[s] + 128 * k : CROW[s] + 128 * k + 128, :].T.astype(BF16)
            for j in range(8):
                piece = block[16 * j : 16 * j + 16]
                if k < 2:
                    ct0[s - 1, :, 256 * j + 128 * k : 256 * j + 128 * k + 128] = piece
                else:
                    ct1[s - 2, :, 128 * j : 128 * j + 128] = piece

    def dense(s, at, width):
        first = CROW[s] + NEAR // 8
        rows_of(first, *((3, 5) if s == LEVELS - 1 else (2, 8)))
        if s == LEVELS - 1:
            c_rows[CROWS : CROWS + 8, :] = jnp.zeros((8, 128), F32)
        wide = dot_t(c_rows[first : first + 128, :].astype(BF16), spread[:, 0:width]) * select[:, 0:width]
        cl[zc, :, at : at + width] = jnp.sum(wide.reshape(8, 16, width), axis=0).astype(BF16)

    for s, (at, end) in enumerate(zip(CL_AT, CL_AT[1:])):
        dense(3 + s, at, end - at)

    wait_factors()
    got = mr[:, 0:48].astype(F32)
    coords = [got[:, 8 * s : 8 * s + 8].reshape(128, 128).astype(BF16) for s in range(4)]
    shapes_lo = got[:, 32:40].reshape(128, 128).astype(BF16)
    shapes_hi = got[:, 40:48].reshape(128, 128).astype(BF16)
    bs[0:8] = dot_t(shapes_lo, coords[0]).reshape(8, 16, 128)
    (b0_send, b0_recv, b1_send, b1_recv, b2_send, b2_recv) = new_sems(6)
    br0[y] = bs[y]
    for k in range(1, NY):
        d = (y + k) % NY
        send(bs.at[d], br0.at[y], b0_send, b0_recv, dev(d, z, c))
    drains.append(lambda: drain(br0.at[pl.ds(0, 7)], b0_send))
    bs[8:12] = dot_t(shapes_hi, coords[1])[0:64].reshape(4, 16, 128)
    br1[y % 4] = bs[8 + y % 4]
    for k in range(1, 4):
        d = (y % 4 + k) % 4
        send(bs.at[8 + d], br1.at[y % 4], b1_send, b1_recv, dev((y // 4) * 4 + d, z, c))
    drains.append(lambda: drain(br1.at[pl.ds(0, 3)], b1_send))
    bs[12:14] = dot_t(shapes_hi, coords[2])[64:96].reshape(2, 16, 128)
    br2[y % 2] = bs[12 + y % 2]
    d = 1 - y % 2
    send(bs.at[12 + d], br2.at[y % 2], b2_send, b2_recv, dev((y // 2) * 2 + d, z, c))
    drains.append(lambda: drain(br2.at[0], b2_send))
    m3[...] = dot_t(shapes_hi, coords[3])[96:112]

    def lookahead(n, d):
        piece = cl.at[zc, :, pl.ds(0, CL_AT[n + 1])]
        return piece, piece

    wait_lookahead = to_row(lookahead, lambda n, count: cl.at[pl.ds(0, count), :, pl.ds(0, CL_AT[n + 1])])

    arrange(1)

    def publish(s, modal):
        value = modal.astype(BF16)
        ny, nz = GROUPS[s]
        known[s][y % ny, z % nz, c] = value
        sv_ref[16 * s : 16 * s + 16, :] = value

    def permute(k_ref, kp):
        rows = kp.shape[0]
        each = rows // 8
        k32[0:rows] = k_ref[...].reshape(rows, 128).astype(F32)
        for j in range(8):
            kp[each * j : each * j + each] = k32[pl.ds(j, each, stride=8), :].astype(BF16)

    def spread_wide(s, during_first, during_second):
        ny, nz = GROUPS[s]
        k_ref = known[s]
        yi, zi = y % ny, z % nz
        y0, z0 = y - yi, z - zi
        (s1, r1, s2, s3, r3) = new_sems(5)
        r2 = new_sems(max(ny, nz) - 1)

        @pl.when(c == 0)
        def _():
            for k in range(1, ny):
                own = k_ref.at[yi, zi, 0]
                send(own, own, s1, r1, dev(y0 + (yi + k) % ny, z, 0))

        @pl.when(c == 1)
        def _():
            for k in range(1, nz):
                own = k_ref.at[yi, zi, 1]
                send(own, own, s1, r1, dev(y, z0 + (zi + k) % nz, 1))

        during_first()

        @pl.when(c == 0)
        def _():
            drain(k_ref.at[pl.ds(0, ny - 1), 0, 0], r1)
            own = k_ref.at[:, zi, 0]
            for k in range(1, nz):
                send(own, own, s2, r2[k - 1], dev(y, z0 + (zi + k) % nz, 0))
            send(own, own, s3, r3, dev(y, z, 1))

        @pl.when(c == 1)
        def _():
            drain(k_ref.at[0, pl.ds(0, nz - 1), 0], r1)
            own = k_ref.at[yi, :, 1]
            for k in range(1, ny):
                send(own, own, s2, r2[k - 1], dev(y0 + (yi + k) % ny, z, 1))
            send(own, own, s3, r3, dev(y, z, 0))

        during_second()

        def nearest(n):
            return sorted(range(1, n), key=lambda k: (min(k, n - k), k))

        @pl.when(c == 0)
        def _():
            for k in nearest(nz):
                piece = k_ref.at[:, (zi + nz - k) % nz, 0]
                drain(piece, r2[k - 1])
                send(piece, piece, s3, r3, dev(y, z, 1))

        @pl.when(c == 1)
        def _():
            for k in nearest(ny):
                piece = k_ref.at[(yi + ny - k) % ny, :, 1]
                drain(piece, r2[k - 1])
                send(piece, piece, s3, r3, dev(y, z, 0))

        drain(k_ref.at[:, :, 0], r3)

        def finish():
            @pl.when(c == 0)
            def _():
                drain(k_ref.at[pl.ds(0, ny - 1), 0, 0], s1)
                drain(k_ref.at[:, pl.ds(0, nz - 1), 0], s2)

            @pl.when(c == 1)
            def _():
                drain(k_ref.at[0, pl.ds(0, nz - 1), 0], s1)
                drain(k_ref.at[pl.ds(0, ny - 1), :, 0], s2)

            drain(k_ref.at[:, :, 0], s3)

        drains.append(finish)

    def spread_half(during):
        yi = y % 4
        (s0, s1, s3, r3) = new_sems(4)
        r1 = new_sems(4)
        own = k1.at[yi, z, c]
        for k in range(4):
            for i in range(1 if k == 0 else 0, NZ):
                send(own, own, s1 if k else s0, r1[k], dev(half + (y + k) % 4, (z + i) % NZ, c))
        during()
        drain(k1.at[0, pl.ds(0, 7), 0], r1[0])
        for k in (0, 1, 3, 2):
            piece = k1.at[(yi + 4 - k) % 4, :, c]
            if k:
                drain(piece, r1[k])
            send(piece, piece, s3, r3, dev(y, z, other))
        drain(k1.at[:, :, 0], r3)

        def finish():
            drain(k1.at[0, pl.ds(0, 7), 0], s0)
            drain(k1.at[pl.ds(0, 3), :, 0], s1)
            drain(k1.at[:, :, 0], s3)

        drains.append(finish)

    def spread_pair(during):
        yi = y % 2
        (s1, r1) = new_sems(2)
        own = kq.at[yi, zc, 0]

        def with_sums(n, d):
            piece = kq.at[yi, zc, pl.ds(0, 2 + n)]
            return piece, piece

        wait_row = to_row(with_sums, lambda n, count: kq.at[0, pl.ds(0, count), pl.ds(0, 2 + n)])
        for k in range(16):
            d = (zc + k) % 16
            send(own, own, s1, r1, dev(mate, d // 2, d % 2))
        during()
        wait_row()
        drain(kq.at[0, :, 0], r1)
        drains.append(lambda: drain(kq.at[0, :, 0], s1))

    def ancestors(block):
        first = k0[...].reshape(2048, 128)
        if block < 2:
            return first[1016 * block : 1016 * block + 1016]
        return jnp.concatenate([first[2032:], k1[...].reshape(1024, 128)[0:1000]], axis=0)

    drain(br0.at[pl.ds(0, 7)], b0_recv)
    publish(0, jnp.sum(br0[...], axis=0))

    def first_0():
        arrange(2)
        quad = mr[pl.ds(base4, 8), 48:64].astype(F32)
        two = mr[pl.ds(base5, 4), 64:80].astype(F32)
        chip = mr[pl.ds(base6, 2), 64:96].astype(F32)

        def part(block, at):
            return block[:, at : at + 8].reshape(-1, 128).astype(BF16)

        m456[0] = dot_t(part(quad, 8), part(quad, 0))
        m456[1] = dot_t(part(two, 8), part(two, 0))
        m456[2] = dot_t(part(chip, 8), part(chip, 16))

    def second_0():
        arrange(3)
        arrange(4)
        by_core(pass_on)

    spread_wide(0, first_0, second_0)

    permute(k0, kp0)
    drain(br1.at[pl.ds(0, 3)], b1_recv)
    publish(1, jnp.sum(br1[...], axis=0) + dot(ct0[0], kp0[...]))

    def during_1():
        arrange(5)
        arrange(6)
        pv[...] = dot(ct0[1:6].reshape(80, 2048), kp0[...]).reshape(5, 16, 128)

    spread_half(during_1)

    permute(k1, kp1)
    drain(br2.at[0], b2_recv)
    product = dot(ct1[...].reshape(80, 1024), kp1[...]) + pv[...].reshape(80, 128)

    def flush(keep):
        while len(drains) > keep:
            drains.pop(0)()

    def own_rows(s, at):
        return m456[s - 4, pl.ds(pl.multiple_of(at, 16), 16), :]

    blocks = (
        product[0:16] + jnp.sum(br2[...], axis=0),
        product[16:32] + m3[...],
        product[32:48] + own_rows(4, near4 * 16),
        product[48:64] + own_rows(5, near5 * 16),
        product[64:80] + own_rows(6, 64 + near6 * 16),
    )
    for n, value in enumerate(blocks):
        kq[y % 2, zc, n] = value.astype(BF16)
    sv_ref[32:48, :] = blocks[0].astype(BF16)

    def during_2():
        lq_copy.wait()
        lphi_copy.wait()
        acc[...] = dot(lq_ref[...], lphi_ref[...])
        cpl_copy.wait()
        by_core(wait_neighbours)
        for block in range(3):
            @pl.when((block + NX - x) % NX != 2)
            def _(block=block):
                acc[...] += dot_t(ancestors(block), cg[block])

        flush(1)

    spread_pair(during_2)

    wait_lookahead()
    above2 = kq[:, :, 0].reshape(512, 128)
    yi = y % 2
    pp3 = kq[yi, :, 1].reshape(256, 128).astype(F32)
    pp4 = kq[yi, pl.ds(base4, 8), 2].reshape(128, 128).astype(F32)
    pp5 = kq[yi, pl.ds(base5, 4), 3].reshape(64, 128).astype(F32)
    pp6 = kq[yi, pl.ds(base6, 2), 4].reshape(32, 128).astype(F32)
    c3 = cl[:, :, CL_AT[0] : CL_AT[1]].reshape(256, 512)
    c4 = cl[pl.ds(base4, 8), :, CL_AT[1] : CL_AT[2]].reshape(128, 768)
    c5 = cl[pl.ds(base5, 4), :, CL_AT[2] : CL_AT[3]].reshape(64, 896)
    c6 = cl[pl.ds(base6, 2), :, CL_AT[3] : CL_AT[4]].reshape(32, 1024)
    first = dot(jnp.concatenate([c3, c4[:, 0:512], c5[:, 0:512], c6[:, 0:512]], axis=0), above2)
    above3 = (pp3 + first[0:256]).astype(BF16)
    second = dot(jnp.concatenate([c4[:, 512:768], c5[:, 512:768], c6[:, 512:768]], axis=0), above3) + first[256:480]
    above4 = (pp4 + second[0:128]).astype(BF16)
    third = dot(jnp.concatenate([c5[:, 768:896], c6[:, 768:896]], axis=0), above4) + second[128:224]
    above5 = (pp5 + third[0:64]).astype(BF16)
    above6 = pp6 + third[64:96] + dot(c6[:, 896:960], above5)
    above6 = above6.astype(BF16)
    k3[...] = above3.reshape(16, 16, 128)
    k4[...] = above4.reshape(8, 16, 128)
    k5[...] = above5.reshape(4, 16, 128)
    k6[...] = above6.reshape(2, 16, 128)
    sv_ref[48:64, :] = k3[zc]
    sv_ref[64:80, :] = k4[near4]
    sv_ref[80:96, :] = k5[near5]
    sv_ref[96:112, :] = k6[near6]

    late = jnp.concatenate(
        [k1[...].reshape(1024, 128)[1000:], above2, above3, above4, above5, above6], axis=0
    )

    @pl.when(x != 1)
    def _():
        acc[...] += dot_t(late, cg[3])

    flush(0)
    by_core(wait_opposite)
    by_core(finish_gather)
    for block in range(NX):
        @pl.when((block + NX - x) % NX == 2)
        def _(block=block):
            acc[...] += dot_t(late if block == 3 else ancestors(block), cg[block])

    total = acc[...]
    live = lax.broadcasted_iota(jnp.int32, (COLS, LEAF), 1) < rows_ref[0]
    out_ref[...] = jnp.where(live, total, 0.0).astype(BF16)


def hand_over(values, leaf, values_out, leaf_out):
    leaf_out[...] = leaf[...]
    values_out[...] = values[...]


N_SEMS = 112


def body(sep_q, sep_phi, coupling, leaf_q, leaf_phi, leaf_coupling, leaf_rows):
    vmem = pl.BlockSpec(memory_space=pltpu.VMEM)
    hbm = pl.BlockSpec(memory_space=pl.ANY)
    block = (16, 128)
    scratch = [
        pltpu.VMEM((56, 128), BF16),
        pltpu.VMEM((8, 4064), BF16),
        pltpu.VMEM((128, 128), BF16),
        pltpu.VMEM((128, LEAF), BF16),
        pltpu.VMEM((1, 328704), BF16),
        pltpu.VMEM((CROWS + 8, 128), F32),
        pltpu.VMEM((128, 1024), BF16),
        pltpu.VMEM((128, 1024), F32),
        pltpu.VMEM((LEVELS - 1, 16, 2048), BF16),
        pltpu.VMEM((LEVELS - 2, 16, 1024), BF16),
        pltpu.VMEM((2048, 128), F32),
        pltpu.VMEM((2048, 128), BF16),
        pltpu.VMEM((1024, 128), BF16),
        pltpu.VMEM((NX, 1016, LEAF), BF16),
        pltpu.VMEM((16, 96, 128), BF16),
        pltpu.VMEM((16, 96, 128), BF16),
        pltpu.VMEM((14,) + block, F32),
        pltpu.VMEM((8,) + block, F32),
        pltpu.VMEM((4,) + block, F32),
        pltpu.VMEM((2,) + block, F32),
        pltpu.VMEM(block, F32),
        pltpu.VMEM((3, 128, 128), F32),
        pltpu.VMEM((16, 16, CL_AT[-1]), BF16),
    ]
    scratch += [pltpu.VMEM(group + (NC,) + block, BF16) for group in GROUPS[:2]]
    scratch += [pltpu.VMEM((2, 16, 5) + block, BF16)]
    scratch += [pltpu.VMEM((n,) + block, BF16) for n in (16, 8, 4, 2)]
    scratch += [
        pltpu.VMEM((LEVELS - 2, 16, 128), F32),
        pltpu.VMEM((COLS, LEAF), F32),
        pltpu.SemaphoreType.DMA((N_SEMS,)),
    ]
    values, leaf = pl.pallas_call(
        kernel,
        out_shape=(
            jax.ShapeDtypeStruct((16 * LEVELS, COLS), BF16),
            jax.ShapeDtypeStruct((COLS, LEAF), BF16),
        ),
        in_specs=[hbm, hbm, hbm, hbm, hbm, hbm, pl.BlockSpec(memory_space=pltpu.SMEM)],
        out_specs=(vmem, vmem),
        scratch_shapes=scratch,
        compiler_params=pltpu.CompilerParams(
            collective_id=0, has_side_effects=True, vmem_limit_bytes=56 * 1024 * 1024
        ),
        cost_estimate=pl.CostEstimate(flops=2_000_000_000, bytes_accessed=4_000_000, transcendentals=0),
    )(sep_q[0].T, sep_phi[0], coupling, leaf_q[0], leaf_phi[0], leaf_coupling[0], leaf_rows)
    values, leaf = pl.pallas_call(
        hand_over,
        out_shape=(
            jax.ShapeDtypeStruct((16 * LEVELS, COLS), BF16),
            jax.ShapeDtypeStruct((COLS, LEAF), BF16),
        ),
        in_specs=[vmem, vmem],
        out_specs=(vmem, vmem),
        compiler_params=pltpu.CompilerParams(vmem_limit_bytes=56 * 1024 * 1024),
    )(values, leaf)
    return values.T[None], leaf[None]


def solution(mesh):
    in_specs = (
        P("sub", "col", None),
        P("sub", None, None),
        P("sub", None),
        P("sub", "col", None),
        P("sub", None, None),
        P("sub", "col", None),
        P("sub"),
    )
    out_specs = (P("sub", "col", None), P("sub", "col", None))
    return jax.shard_map(body, mesh=mesh, in_specs=in_specs, out_specs=out_specs, check_vma=False)
```

```python
import jax
import jax.numpy as jnp
from jax import lax
from jax.experimental import pallas as pl
from jax.experimental.pallas import tpu as pltpu
from jax.sharding import PartitionSpec as P

MESH = pl.DeviceIdType.MESH
F32 = jnp.float32
BF16 = jnp.bfloat16
NY, NZ, NC, NX = 8, 8, 2, 4
COLS = 128
LEAF = 640
GROUPS = ((8, 8), (4, 8), (2, 8), (1, 8), (1, 4), (1, 2), (1, 1))
LEVELS = len(GROUPS)
CROW = (0, 0, 256, 640, 1088, 1568, 2064)
NEAR = 3072
CL_AT = (0, 512, 1280, 2176, 3200)
CROWS = 2568


def dot_t(a, b):
    return lax.dot_general(a, b, (((0,), (0,)), ((), ())), preferred_element_type=F32)


def dot(a, b):
    return jnp.dot(a, b, preferred_element_type=F32)


def kernel(
    q_hbm, phi_hbm, c_hbm, lq_hbm, lphi_hbm, cpl_hbm, rows_ref,
    sv_ref, out_ref,
    q_ref, phi_ref, lq_ref, lphi_ref, c_flat, c_rows, spread, select, ct0, ct1, k32, kp0, kp1, cg,
    ms, mr, bs, br0, br1, br2, m3, m456, cl,
    k0, k1, kq, k3, k4, k5, k6, pv, acc,
    sems,
):
    known = (k0, k1)
    sub = lax.axis_index("sub")
    x = lax.axis_index("col")
    y, z, c = sub // 16, (sub // 2) % 8, sub % 2
    other = 1 - c
    zc = z * 2 + c
    zq = (z % 4) * 2 + c

    counter = [0]

    def new_sems(n):
        first = counter[0]
        counter[0] += n
        return [sems.at[first + i] for i in range(n)]

    def dev(y_, z_, c_):
        return ((y_ * 8 + z_) * 2 + c_, x)

    def send(src, dst, ss, rs, target):
        pltpu.make_async_remote_copy(
            src_ref=src, dst_ref=dst, send_sem=ss, recv_sem=rs,
            device_id=target, device_id_type=MESH,
        ).start()

    def drain(like, sem):
        pltpu.make_async_copy(like, like, sem).wait()

    drains = []

    fetches = []
    for src, dst, sem in zip(
        (q_hbm, phi_hbm, c_hbm, cpl_hbm, lq_hbm, lphi_hbm),
        (q_ref, phi_ref, c_flat, cg.at[x], lq_ref, lphi_ref),
        new_sems(6),
    ):
        fetches.append(pltpu.make_async_copy(src, dst, sem))
    q_copy, phi_copy, c_copy, cpl_copy, lq_copy, lphi_copy = fetches
    q_copy.start()
    phi_copy.start()

    barrier = pltpu.get_barrier_semaphore()
    for k in range(1, 16):
        d = (zc + k) % 16
        pl.semaphore_signal(barrier, inc=1, device_id=dev(y, d // 2, d % 2), device_id_type=MESH)
    half, pair = (y // 4) * 4, (y // 2) * 2
    mate = 2 * pair + 1 - y
    for k in range(1, 4):
        for i in range(NZ):
            pl.semaphore_signal(barrier, inc=1, device_id=dev(half + (y + k) % 4, i, c), device_id_type=MESH)
    for i in range(NZ):
        pl.semaphore_signal(barrier, inc=1, device_id=dev(mate, i, other), device_id_type=MESH)
    for k in range(4):
        pl.semaphore_signal(barrier, inc=1, device_id=dev(4 - half + k, z, c), device_id_type=MESH)
    for k in (1, NX - 1):
        pl.semaphore_signal(barrier, inc=1, device_id=(sub, (x + k) % NX), device_id_type=MESH)

    for fetch in (c_copy, cpl_copy, lq_copy, lphi_copy):
        fetch.start()

    q_copy.wait()
    phi_copy.wait()
    phi = phi_ref[...].astype(F32)
    qf = q_ref[...].astype(F32)
    lane = lax.broadcasted_iota(jnp.int32, (8, 128), 1)
    zero = jnp.zeros((8, 128), F32)
    shared = [
        qf[32:40],
        phi[:, 3840:3968],
        qf[40:48],
        jnp.concatenate([phi[:, 3968:4064], zero[:, 0:32]], axis=1),
        qf[48:56],
        zero,
    ]
    for d in range(16):
        h, p = divmod(d, 8)
        parts = [qf[0:32]]
        for g in range(2):
            piece = jnp.zeros((8, 128), F32)
            for b in range(8 * g, min(8 * g + 8, 15)):
                block = phi[:, b * 256 + h * 128 : b * 256 + h * 128 + 128]
                shift = ((b % 8 - p) * 16) % 128
                if shift:
                    block = pltpu.roll(block, shift, 1)
                piece = jnp.where(lax.shift_right_logical(lane, 4) == b % 8, block, piece)
            parts.append(piece)
        ms[d] = jnp.concatenate(parts + shared, axis=0).astype(BF16)
    mr[zc] = ms[zc]

    pl.semaphore_wait(barrier, 15 + 24 + 8 + 4 + 2)

    pieces = (pl.ds(0, 512), pl.ds(512, 504))
    left, right = (x + NX - 1) % NX, (x + 1) % NX
    (gr_send, gl_send, fr_send, fl_send, l0, l1, r0, r1, o_l, o_r) = new_sems(10)

    def by_core(step):
        for core in range(NC):
            @pl.when(c == core)
            def _(core=core):
                step(pieces[core], pieces[1 - core])

    def give(one, two):
        for part, rs_right in ((one, l0), (two, l1)):
            send(cpl_hbm.at[part], cg.at[x, part], gr_send, rs_right, (sub, right))
        for part, rs_left in ((two, r0), (one, r1)):
            send(cpl_hbm.at[part], cg.at[x, part], gl_send, rs_left, (sub, left))

    def pass_on(one, two):
        piece = cg.at[left, one]
        drain(piece, l0)
        send(piece, piece, fr_send, o_l, (sub, right))
        piece = cg.at[right, two]
        drain(piece, r0)
        send(piece, piece, fl_send, o_r, (sub, left))

    def wait_neighbours(one, two):
        drain(cg.at[0, two], l1)
        drain(cg.at[0, one], r1)

    def wait_opposite(one, two):
        drain(cg.at[0, one], o_l)
        drain(cg.at[0, two], o_r)

    def finish_gather(one, two):
        drain(cg.at[0], gr_send)
        drain(cg.at[0], gl_send)
        drain(cg.at[0, one], fr_send)
        drain(cg.at[0, two], fl_send)

    by_core(give)

    base4, base5, base6 = zc - zq, zc - zc % 4, zc - c
    near4, near5, near6 = zq, zc % 4, c
    classes = (
        [8 - base4 + (near4 + i) % 8 for i in range(8)],
        [base4 + 4 - (base5 - base4) + (near5 + i) % 4 for i in range(4)],
        [base5 + 2 - (base6 - base5) + (near6 + i) % 2 for i in range(2)],
        [base6 + other],
    )

    def to_row(source, like):
        ss, rs = new_sems(4), new_sems(4)
        for n, places in enumerate(classes):
            for d in places:
                src, dst = source(n, d)
                send(src, dst, ss[n], rs[n], dev(y, d // 2, d % 2))

        def wait(sems_):
            for n, places in enumerate(classes):
                drain(like(n, len(places)), sems_[n])

        drains.append(lambda: wait(ss))
        return lambda: wait(rs)

    def factors(n, d):
        return ms.at[d, pl.ds(0, 48 + 16 * n)], mr.at[zc, pl.ds(0, 48 + 16 * n)]

    wait_factors = to_row(factors, lambda n, count: mr.at[pl.ds(0, count), pl.ds(0, 48 + 16 * n)])

    c_copy.wait()
    wide_row = lax.broadcasted_iota(jnp.int32, (128, 1024), 0)
    wide_col = lax.broadcasted_iota(jnp.int32, (128, 1024), 1)
    spread[...] = jnp.where(lax.shift_right_logical(wide_col, 3) == wide_row, 1.0, 0.0).astype(BF16)
    select[...] = jnp.where((wide_col & 7) == lax.shift_right_logical(wide_row, 4), 1.0, 0.0)

    def rows_of(first, steps, each):
        def step(i, carry):
            for k in range(each):
                row = pl.multiple_of(first + (i * each + k) * 8, 8)
                at = pl.multiple_of(row * 128, 1024)
                value = c_flat[0:1, pl.ds(at, 1024)].astype(F32).reshape(8, 128)
                c_rows[pl.ds(row, 8), :] = value
            return carry

        lax.fori_loop(0, steps, step, 0)

    def arrange(s):
        rows_of(CROW[s], 4 if s == 1 else 6, 8)
        for k in range(2 if s == 1 else 3):
            block = c_rows[CROW[s] + 128 * k : CROW[s] + 128 * k + 128, :].T.astype(BF16)
            for j in range(8):
                piece = block[16 * j : 16 * j + 16]
                if k < 2:
                    ct0[s - 1, :, 256 * j + 128 * k : 256 * j + 128 * k + 128] = piece
                else:
                    ct1[s - 2, :, 128 * j : 128 * j + 128] = piece

    def dense(s, at, width):
        first = CROW[s] + NEAR // 8
        rows_of(first, *((3, 5) if s == LEVELS - 1 else (2, 8)))
        if s == LEVELS - 1:
            c_rows[CROWS : CROWS + 8, :] = jnp.zeros((8, 128), F32)
        wide = dot_t(c_rows[first : first + 128, :].astype(BF16), spread[:, 0:width]) * select[:, 0:width]
        cl[zc, :, at : at + width] = jnp.sum(wide.reshape(8, 16, width), axis=0).astype(BF16)

    for s, (at, end) in enumerate(zip(CL_AT, CL_AT[1:])):
        dense(3 + s, at, end - at)

    wait_factors()
    got = mr[:, 0:48].astype(F32)
    coords = [got[:, 8 * s : 8 * s + 8].reshape(128, 128).astype(BF16) for s in range(4)]
    shapes_lo = got[:, 32:40].reshape(128, 128).astype(BF16)
    shapes_hi = got[:, 40:48].reshape(128, 128).astype(BF16)
    bs[0:8] = dot_t(shapes_lo, coords[0]).reshape(8, 16, 128)
    (b0_send, b0_recv, b1_send, b1_recv, b2_send, b2_recv) = new_sems(6)
    br0[y] = bs[y]
    for k in range(1, NY):
        d = (y + k) % NY
        send(bs.at[d], br0.at[y], b0_send, b0_recv, dev(d, z, c))
    drains.append(lambda: drain(br0.at[pl.ds(0, 7)], b0_send))
    bs[8:12] = dot_t(shapes_hi, coords[1])[0:64].reshape(4, 16, 128)
    br1[y % 4] = bs[8 + y % 4]
    for k in range(1, 4):
        d = (y % 4 + k) % 4
        send(bs.at[8 + d], br1.at[y % 4], b1_send, b1_recv, dev((y // 4) * 4 + d, z, c))
    drains.append(lambda: drain(br1.at[pl.ds(0, 3)], b1_send))
    bs[12:14] = dot_t(shapes_hi, coords[2])[64:96].reshape(2, 16, 128)
    br2[y % 2] = bs[12 + y % 2]
    d = 1 - y % 2
    send(bs.at[12 + d], br2.at[y % 2], b2_send, b2_recv, dev((y // 2) * 2 + d, z, c))
    drains.append(lambda: drain(br2.at[0], b2_send))
    m3[...] = dot_t(shapes_hi, coords[3])[96:112]

    def lookahead(n, d):
        piece = cl.at[zc, :, pl.ds(0, CL_AT[n + 1])]
        return piece, piece

    wait_lookahead = to_row(lookahead, lambda n, count: cl.at[pl.ds(0, count), :, pl.ds(0, CL_AT[n + 1])])

    arrange(1)

    def publish(s, modal):
        value = modal.astype(BF16)
        ny, nz = GROUPS[s]
        known[s][y % ny, z % nz, c] = value
        sv_ref[16 * s : 16 * s + 16, :] = value

    def permute(k_ref, kp):
        rows = kp.shape[0]
        each = rows // 8
        k32[0:rows] = k_ref[...].reshape(rows, 128).astype(F32)
        for j in range(8):
            kp[each * j : each * j + each] = k32[pl.ds(j, each, stride=8), :].astype(BF16)

    def spread_wide(s, during_first, during_second):
        ny, nz = GROUPS[s]
        k_ref = known[s]
        yi, zi = y % ny, z % nz
        y0, z0 = y - yi, z - zi
        (s1, r1, s2, s3, r3) = new_sems(5)
        r2 = new_sems(max(ny, nz) - 1)

        @pl.when(c == 0)
        def _():
            for k in range(1, ny):
                own = k_ref.at[yi, zi, 0]
                send(own, own, s1, r1, dev(y0 + (yi + k) % ny, z, 0))

        @pl.when(c == 1)
        def _():
            for k in range(1, nz):
                own = k_ref.at[yi, zi, 1]
                send(own, own, s1, r1, dev(y, z0 + (zi + k) % nz, 1))

        during_first()

        @pl.when(c == 0)
        def _():
            drain(k_ref.at[pl.ds(0, ny - 1), 0, 0], r1)
            own = k_ref.at[:, zi, 0]
            for k in range(1, nz):
                send(own, own, s2, r2[k - 1], dev(y, z0 + (zi + k) % nz, 0))
            send(own, own, s3, r3, dev(y, z, 1))

        @pl.when(c == 1)
        def _():
            drain(k_ref.at[0, pl.ds(0, nz - 1), 0], r1)
            own = k_ref.at[yi, :, 1]
            for k in range(1, ny):
                send(own, own, s2, r2[k - 1], dev(y0 + (yi + k) % ny, z, 1))
            send(own, own, s3, r3, dev(y, z, 0))

        during_second()

        def nearest(n):
            return sorted(range(1, n), key=lambda k: (min(k, n - k), k))

        @pl.when(c == 0)
        def _():
            for k in nearest(nz):
                piece = k_ref.at[:, (zi + nz - k) % nz, 0]
                drain(piece, r2[k - 1])
                send(piece, piece, s3, r3, dev(y, z, 1))

        @pl.when(c == 1)
        def _():
            for k in nearest(ny):
                piece = k_ref.at[(yi + ny - k) % ny, :, 1]
                drain(piece, r2[k - 1])
                send(piece, piece, s3, r3, dev(y, z, 0))

        drain(k_ref.at[:, :, 0], r3)

        def finish():
            @pl.when(c == 0)
            def _():
                drain(k_ref.at[pl.ds(0, ny - 1), 0, 0], s1)
                drain(k_ref.at[:, pl.ds(0, nz - 1), 0], s2)

            @pl.when(c == 1)
            def _():
                drain(k_ref.at[0, pl.ds(0, nz - 1), 0], s1)
                drain(k_ref.at[pl.ds(0, ny - 1), :, 0], s2)

            drain(k_ref.at[:, :, 0], s3)

        drains.append(finish)

    def spread_half(during):
        yi = y % 4
        (s0, s1, s3, r3) = new_sems(4)
        r1 = new_sems(4)
        own = k1.at[yi, z, c]
        for k in range(4):
            for i in range(1 if k == 0 else 0, NZ):
                send(own, own, s1 if k else s0, r1[k], dev(half + (y + k) % 4, (z + i) % NZ, c))
        during()
        drain(k1.at[0, pl.ds(0, 7), 0], r1[0])
        for k in (0, 1, 3, 2):
            piece = k1.at[(yi + 4 - k) % 4, :, c]
            if k:
                drain(piece, r1[k])
            send(piece, piece, s3, r3, dev(y, z, other))
        drain(k1.at[:, :, 0], r3)

        def finish():
            drain(k1.at[0, pl.ds(0, 7), 0], s0)
            drain(k1.at[pl.ds(0, 3), :, 0], s1)
            drain(k1.at[:, :, 0], s3)

        drains.append(finish)

    def spread_pair(during):
        yi = y % 2
        (s1, r1) = new_sems(2)
        own = kq.at[yi, zc, 0]

        def with_sums(n, d):
            piece = kq.at[yi, zc, pl.ds(0, 2 + n)]
            return piece, piece

        wait_row = to_row(with_sums, lambda n, count: kq.at[0, pl.ds(0, count), pl.ds(0, 2 + n)])
        for k in range(16):
            d = (zc + k) % 16
            send(own, own, s1, r1, dev(mate, d // 2, d % 2))
        during()
        wait_row()
        drain(kq.at[0, :, 0], r1)
        drains.append(lambda: drain(kq.at[0, :, 0], s1))

    def ancestors(block):
        first = k0[...].reshape(2048, 128)
        if block < 2:
            return first[1016 * block : 1016 * block + 1016]
        return jnp.concatenate([first[2032:], k1[...].reshape(1024, 128)[0:1000]], axis=0)

    drain(br0.at[pl.ds(0, 7)], b0_recv)
    publish(0, jnp.sum(br0[...], axis=0))

    def first_0():
        arrange(2)
        quad = mr[pl.ds(base4, 8), 48:64].astype(F32)
        two = mr[pl.ds(base5, 4), 64:80].astype(F32)
        chip = mr[pl.ds(base6, 2), 64:96].astype(F32)

        def part(block, at):
            return block[:, at : at + 8].reshape(-1, 128).astype(BF16)

        m456[0] = dot_t(part(quad, 8), part(quad, 0))
        m456[1] = dot_t(part(two, 8), part(two, 0))
        m456[2] = dot_t(part(chip, 8), part(chip, 16))

    def second_0():
        arrange(3)
        arrange(4)
        by_core(pass_on)

    spread_wide(0, first_0, second_0)

    permute(k0, kp0)
    drain(br1.at[pl.ds(0, 3)], b1_recv)
    publish(1, jnp.sum(br1[...], axis=0) + dot(ct0[0], kp0[...]))

    def during_1():
        arrange(5)
        arrange(6)
        pv[...] = dot(ct0[1:6].reshape(80, 2048), kp0[...]).reshape(5, 16, 128)

    spread_half(during_1)

    permute(k1, kp1)
    drain(br2.at[0], b2_recv)
    product = dot(ct1[...].reshape(80, 1024), kp1[...]) + pv[...].reshape(80, 128)

    def flush(keep):
        while len(drains) > keep:
            drains.pop(0)()

    def own_rows(s, at):
        return m456[s - 4, pl.ds(pl.multiple_of(at, 16), 16), :]

    blocks = (
        product[0:16] + jnp.sum(br2[...], axis=0),
        product[16:32] + m3[...],
        product[32:48] + own_rows(4, near4 * 16),
        product[48:64] + own_rows(5, near5 * 16),
        product[64:80] + own_rows(6, 64 + near6 * 16),
    )
    for n, value in enumerate(blocks):
        kq[y % 2, zc, n] = value.astype(BF16)
    sv_ref[32:48, :] = blocks[0].astype(BF16)

    def during_2():
        lq_copy.wait()
        lphi_copy.wait()
        acc[...] = dot(lq_ref[...], lphi_ref[...])
        cpl_copy.wait()
        by_core(wait_neighbours)
        for block in range(3):
            @pl.when((block + NX - x) % NX != 2)
            def _(block=block):
                acc[...] += dot_t(ancestors(block), cg[block])

        flush(1)

    spread_pair(during_2)

    wait_lookahead()
    above2 = kq[:, :, 0].reshape(512, 128)
    yi = y % 2
    pp3 = kq[yi, :, 1].reshape(256, 128).astype(F32)
    pp4 = kq[yi, pl.ds(base4, 8), 2].reshape(128, 128).astype(F32)
    pp5 = kq[yi, pl.ds(base5, 4), 3].reshape(64, 128).astype(F32)
    pp6 = kq[yi, pl.ds(base6, 2), 4].reshape(32, 128).astype(F32)
    c3 = cl[:, :, CL_AT[0] : CL_AT[1]].reshape(256, 512)
    c4 = cl[pl.ds(base4, 8), :, CL_AT[1] : CL_AT[2]].reshape(128, 768)
    c5 = cl[pl.ds(base5, 4), :, CL_AT[2] : CL_AT[3]].reshape(64, 896)
    c6 = cl[pl.ds(base6, 2), :, CL_AT[3] : CL_AT[4]].reshape(32, 1024)
    first = dot(jnp.concatenate([c3, c4[:, 0:512], c5[:, 0:512], c6[:, 0:512]], axis=0), above2)
    above3 = (pp3 + first[0:256]).astype(BF16)
    second = dot(jnp.concatenate([c4[:, 512:768], c5[:, 512:768], c6[:, 512:768]], axis=0), above3) + first[256:480]
    above4 = (pp4 + second[0:128]).astype(BF16)
    third = dot(jnp.concatenate([c5[:, 768:896], c6[:, 768:896]], axis=0), above4) + second[128:224]
    above5 = (pp5 + third[0:64]).astype(BF16)
    above6 = pp6 + third[64:96] + dot(c6[:, 896:960], above5)
    above6 = above6.astype(BF16)
    k3[...] = above3.reshape(16, 16, 128)
    k4[...] = above4.reshape(8, 16, 128)
    k5[...] = above5.reshape(4, 16, 128)
    k6[...] = above6.reshape(2, 16, 128)
    sv_ref[48:64, :] = k3[zc]
    sv_ref[64:80, :] = k4[near4]
    sv_ref[80:96, :] = k5[near5]
    sv_ref[96:112, :] = k6[near6]

    late = jnp.concatenate(
        [k1[...].reshape(1024, 128)[1000:], above2, above3, above4, above5, above6], axis=0
    )

    @pl.when(x != 1)
    def _():
        acc[...] += dot_t(late, cg[3])

    flush(0)
    by_core(wait_opposite)
    by_core(finish_gather)
    for block in range(NX):
        @pl.when((block + NX - x) % NX == 2)
        def _(block=block):
            acc[...] += dot_t(late if block == 3 else ancestors(block), cg[block])

    total = acc[...]
    live = lax.broadcasted_iota(jnp.int32, (COLS, LEAF), 1) < rows_ref[0]
    out_ref[...] = jnp.where(live, total, 0.0).astype(BF16)


def hand_over(values, leaf, values_out, leaf_out):
    leaf_out[...] = leaf[...]
    values_out[...] = values[...]


N_SEMS = 112


def body(sep_q, sep_phi, coupling, leaf_q, leaf_phi, leaf_coupling, leaf_rows):
    vmem = pl.BlockSpec(memory_space=pltpu.VMEM)
    hbm = pl.BlockSpec(memory_space=pl.ANY)
    block = (16, 128)
    scratch = [
        pltpu.VMEM((56, 128), BF16),
        pltpu.VMEM((8, 4064), BF16),
        pltpu.VMEM((128, 128), BF16),
        pltpu.VMEM((128, LEAF), BF16),
        pltpu.VMEM((1, 328704), BF16),
        pltpu.VMEM((CROWS + 8, 128), F32),
        pltpu.VMEM((128, 1024), BF16),
        pltpu.VMEM((128, 1024), F32),
        pltpu.VMEM((LEVELS - 1, 16, 2048), BF16),
        pltpu.VMEM((LEVELS - 2, 16, 1024), BF16),
        pltpu.VMEM((2048, 128), F32),
        pltpu.VMEM((2048, 128), BF16),
        pltpu.VMEM((1024, 128), BF16),
        pltpu.VMEM((NX, 1016, LEAF), BF16),
        pltpu.VMEM((16, 96, 128), BF16),
        pltpu.VMEM((16, 96, 128), BF16),
        pltpu.VMEM((14,) + block, F32),
        pltpu.VMEM((8,) + block, F32),
        pltpu.VMEM((4,) + block, F32),
        pltpu.VMEM((2,) + block, F32),
        pltpu.VMEM(block, F32),
        pltpu.VMEM((3, 128, 128), F32),
        pltpu.VMEM((16, 16, CL_AT[-1]), BF16),
    ]
    scratch += [pltpu.VMEM(group + (NC,) + block, BF16) for group in GROUPS[:2]]
    scratch += [pltpu.VMEM((2, 16, 5) + block, BF16)]
    scratch += [pltpu.VMEM((n,) + block, BF16) for n in (16, 8, 4, 2)]
    scratch += [
        pltpu.VMEM((LEVELS - 2, 16, 128), F32),
        pltpu.VMEM((COLS, LEAF), F32),
        pltpu.SemaphoreType.DMA((N_SEMS,)),
    ]
    values, leaf = pl.pallas_call(
        kernel,
        out_shape=(
            jax.ShapeDtypeStruct((16 * LEVELS, COLS), BF16),
            jax.ShapeDtypeStruct((COLS, LEAF), BF16),
        ),
        in_specs=[hbm, hbm, hbm, hbm, hbm, hbm, pl.BlockSpec(memory_space=pltpu.SMEM)],
        out_specs=(vmem, vmem),
        scratch_shapes=scratch,
        compiler_params=pltpu.CompilerParams(
            collective_id=0, has_side_effects=True, vmem_limit_bytes=56 * 1024 * 1024
        ),
        cost_estimate=pl.CostEstimate(flops=2_000_000_000, bytes_accessed=4_000_000, transcendentals=0),
    )(sep_q[0].T, sep_phi[0], coupling, leaf_q[0], leaf_phi[0], leaf_coupling[0], leaf_rows)
    values, leaf = pl.pallas_call(
        hand_over,
        out_shape=(
            jax.ShapeDtypeStruct((16 * LEVELS, COLS), BF16),
            jax.ShapeDtypeStruct((COLS, LEAF), BF16),
        ),
        in_specs=[vmem, vmem],
        out_specs=(vmem, vmem),
        compiler_params=pltpu.CompilerParams(vmem_limit_bytes=56 * 1024 * 1024),
    )(values, leaf)
    return values.T[None], leaf[None]


def solution(mesh):
    in_specs = (
        P("sub", "col", None),
        P("sub", None, None),
        P("sub", None),
        P("sub", "col", None),
        P("sub", None, None),
        P("sub", "col", None),
        P("sub"),
    )
    out_specs = (P("sub", "col", None), P("sub", "col", None))
    return jax.shard_map(body, mesh=mesh, in_specs=in_specs, out_specs=out_specs, check_vma=False)
```

```python
import jax
import jax.numpy as jnp
from jax import lax
from jax.experimental import pallas as pl
from jax.experimental.pallas import tpu as pltpu
from jax.sharding import PartitionSpec as P

MESH = pl.DeviceIdType.MESH
F32 = jnp.float32
BF16 = jnp.bfloat16
NY, NZ, NC, NX = 8, 8, 2, 4
COLS = 128
LEAF = 640
GROUPS = ((8, 8), (4, 8), (2, 8), (1, 8), (1, 4), (1, 2), (1, 1))
LEVELS = len(GROUPS)
CROW = (0, 0, 256, 640, 1088, 1568, 2064)
NEAR = 3072
CL_AT = (0, 512, 1280, 2176, 3200)
CROWS = 2568


def dot_t(a, b):
    return lax.dot_general(a, b, (((0,), (0,)), ((), ())), preferred_element_type=F32)


def dot(a, b):
    return jnp.dot(a, b, preferred_element_type=F32)


def kernel(
    q_hbm, phi_hbm, c_hbm, lq_hbm, lphi_hbm, cpl_hbm, rows_ref,
    sv_ref, out_ref,
    q_ref, phi_ref, lq_ref, lphi_ref, c_flat, c_rows, spread, select, ct0, ct1, k32, kp0, kp1, cg,
    ms, mr, bs, br0, br1, br2, m3, m456, cl,
    k0, k1, kq, k3, k4, k5, k6, pv, acc,
    sems,
):
    known = (k0, k1)
    sub = lax.axis_index("sub")
    x = lax.axis_index("col")
    y, z, c = sub // 16, (sub // 2) % 8, sub % 2
    other = 1 - c
    zc = z * 2 + c
    zq = (z % 4) * 2 + c

    counter = [0]

    def new_sems(n):
        first = counter[0]
        counter[0] += n
        return [sems.at[first + i] for i in range(n)]

    def dev(y_, z_, c_):
        return ((y_ * 8 + z_) * 2 + c_, x)

    def send(src, dst, ss, rs, target):
        pltpu.make_async_remote_copy(
            src_ref=src, dst_ref=dst, send_sem=ss, recv_sem=rs,
            device_id=target, device_id_type=MESH,
        ).start()

    def drain(like, sem):
        pltpu.make_async_copy(like, like, sem).wait()

    drains = []

    fetches = []
    for src, dst, sem in zip(
        (q_hbm, phi_hbm, c_hbm, cpl_hbm, lq_hbm, lphi_hbm),
        (q_ref, phi_ref, c_flat, cg.at[x], lq_ref, lphi_ref),
        new_sems(6),
    ):
        fetches.append(pltpu.make_async_copy(src, dst, sem))
    q_copy, phi_copy, c_copy, cpl_copy, lq_copy, lphi_copy = fetches
    q_copy.start()
    phi_copy.start()

    barrier = pltpu.get_barrier_semaphore()
    for k in range(1, 16):
        d = (zc + k) % 16
        pl.semaphore_signal(barrier, inc=1, device_id=dev(y, d // 2, d % 2), device_id_type=MESH)
    half, pair = (y // 4) * 4, (y // 2) * 2
    mate = 2 * pair + 1 - y
    for k in range(1, 4):
        for i in range(NZ):
            pl.semaphore_signal(barrier, inc=1, device_id=dev(half + (y + k) % 4, i, c), device_id_type=MESH)
    for i in range(NZ):
        pl.semaphore_signal(barrier, inc=1, device_id=dev(mate, i, other), device_id_type=MESH)
    for k in range(4):
        pl.semaphore_signal(barrier, inc=1, device_id=dev(4 - half + k, z, c), device_id_type=MESH)
    for k in (1, NX - 1):
        pl.semaphore_signal(barrier, inc=1, device_id=(sub, (x + k) % NX), device_id_type=MESH)

    for fetch in (c_copy, cpl_copy, lq_copy, lphi_copy):
        fetch.start()

    q_copy.wait()
    phi_copy.wait()
    phi = phi_ref[...].astype(F32)
    qf = q_ref[...].astype(F32)
    lane = lax.broadcasted_iota(jnp.int32, (8, 128), 1)
    zero = jnp.zeros((8, 128), F32)
    shared = [
        qf[32:40],
        phi[:, 3840:3968],
        qf[40:48],
        jnp.concatenate([phi[:, 3968:4064], zero[:, 0:32]], axis=1),
        qf[48:56],
        zero,
    ]
    for d in range(16):
        h, p = divmod(d, 8)
        parts = [qf[0:32]]
        for g in range(2):
            piece = jnp.zeros((8, 128), F32)
            for b in range(8 * g, min(8 * g + 8, 15)):
                block = phi[:, b * 256 + h * 128 : b * 256 + h * 128 + 128]
                shift = ((b % 8 - p) * 16) % 128
                if shift:
                    block = pltpu.roll(block, shift, 1)
                piece = jnp.where(lax.shift_right_logical(lane, 4) == b % 8, block, piece)
            parts.append(piece)
        ms[d] = jnp.concatenate(parts + shared, axis=0).astype(BF16)
    mr[zc] = ms[zc]

    pl.semaphore_wait(barrier, 15 + 24 + 8 + 4 + 2)

    pieces = (pl.ds(0, 512), pl.ds(512, 504))
    left, right = (x + NX - 1) % NX, (x + 1) % NX
    (gr_send, gl_send, fr_send, fl_send, l0, l1, r0, r1, o_l, o_r) = new_sems(10)

    def by_core(step):
        for core in range(NC):
            @pl.when(c == core)
            def _(core=core):
                step(pieces[core], pieces[1 - core])

    def give(one, two):
        for part, rs_right in ((one, l0), (two, l1)):
            send(cpl_hbm.at[part], cg.at[x, part], gr_send, rs_right, (sub, right))
        for part, rs_left in ((two, r0), (one, r1)):
            send(cpl_hbm.at[part], cg.at[x, part], gl_send, rs_left, (sub, left))

    def pass_on(one, two):
        piece = cg.at[left, one]
        drain(piece, l0)
        send(piece, piece, fr_send, o_l, (sub, right))
        piece = cg.at[right, two]
        drain(piece, r0)
        send(piece, piece, fl_send, o_r, (sub, left))

    def wait_neighbours(one, two):
        drain(cg.at[0, two], l1)
        drain(cg.at[0, one], r1)

    def wait_opposite(one, two):
        drain(cg.at[0, one], o_l)
        drain(cg.at[0, two], o_r)

    def finish_gather(one, two):
        drain(cg.at[0], gr_send)
        drain(cg.at[0], gl_send)
        drain(cg.at[0, one], fr_send)
        drain(cg.at[0, two], fl_send)

    by_core(give)

    base4, base5, base6 = zc - zq, zc - zc % 4, zc - c
    near4, near5, near6 = zq, zc % 4, c
    classes = (
        [8 - base4 + (near4 + i) % 8 for i in range(8)],
        [base4 + 4 - (base5 - base4) + (near5 + i) % 4 for i in range(4)],
        [base5 + 2 - (base6 - base5) + (near6 + i) % 2 for i in range(2)],
        [base6 + other],
    )

    def to_row(source, like):
        ss, rs = new_sems(4), new_sems(4)
        for n, places in enumerate(classes):
            for d in places:
                src, dst = source(n, d)
                send(src, dst, ss[n], rs[n], dev(y, d // 2, d % 2))

        def wait(sems_):
            for n, places in enumerate(classes):
                drain(like(n, len(places)), sems_[n])

        drains.append(lambda: wait(ss))
        return lambda: wait(rs)

    def factors(n, d):
        return ms.at[d, pl.ds(0, 48 + 16 * n)], mr.at[zc, pl.ds(0, 48 + 16 * n)]

    wait_factors = to_row(factors, lambda n, count: mr.at[pl.ds(0, count), pl.ds(0, 48 + 16 * n)])

    c_copy.wait()
    wide_row = lax.broadcasted_iota(jnp.int32, (128, 1024), 0)
    wide_col = lax.broadcasted_iota(jnp.int32, (128, 1024), 1)
    spread[...] = jnp.where(lax.shift_right_logical(wide_col, 3) == wide_row, 1.0, 0.0).astype(BF16)
    select[...] = jnp.where((wide_col & 7) == lax.shift_right_logical(wide_row, 4), 1.0, 0.0)

    def rows_of(first, steps, each):
        def step(i, carry):
            for k in range(each):
                row = pl.multiple_of(first + (i * each + k) * 8, 8)
                at = pl.multiple_of(row * 128, 1024)
                value = c_flat[0:1, pl.ds(at, 1024)].astype(F32).reshape(8, 128)
                c_rows[pl.ds(row, 8), :] = value
            return carry

        lax.fori_loop(0, steps, step, 0)

    def arrange(s):
        rows_of(CROW[s], 4 if s == 1 else 6, 8)
        for k in range(2 if s == 1 else 3):
            block = c_rows[CROW[s] + 128 * k : CROW[s] + 128 * k + 128, :].T.astype(BF16)
            for j in range(8):
                piece = block[16 * j : 16 * j + 16]
                if k < 2:
                    ct0[s - 1, :, 256 * j + 128 * k : 256 * j + 128 * k + 128] = piece
                else:
                    ct1[s - 2, :, 128 * j : 128 * j + 128] = piece

    def dense(s, at, width):
        first = CROW[s] + NEAR // 8
        rows_of(first, *((3, 5) if s == LEVELS - 1 else (2, 8)))
        if s == LEVELS - 1:
            c_rows[CROWS : CROWS + 8, :] = jnp.zeros((8, 128), F32)
        wide = dot_t(c_rows[first : first + 128, :].astype(BF16), spread[:, 0:width]) * select[:, 0:width]
        cl[zc, :, at : at + width] = jnp.sum(wide.reshape(8, 16, width), axis=0).astype(BF16)

    for s, (at, end) in enumerate(zip(CL_AT, CL_AT[1:])):
        dense(3 + s, at, end - at)

    wait_factors()
    got = mr[:, 0:48].astype(F32)
    coords = [got[:, 8 * s : 8 * s + 8].reshape(128, 128).astype(BF16) for s in range(4)]
    shapes_lo = got[:, 32:40].reshape(128, 128).astype(BF16)
    shapes_hi = got[:, 40:48].reshape(128, 128).astype(BF16)
    bs[0:8] = dot_t(shapes_lo, coords[0]).reshape(8, 16, 128)
    (b0_send, b0_recv, b1_send, b1_recv, b2_send, b2_recv) = new_sems(6)
    br0[y] = bs[y]
    for k in range(1, NY):
        d = (y + k) % NY
        send(bs.at[d], br0.at[y], b0_send, b0_recv, dev(d, z, c))
    drains.append(lambda: drain(br0.at[pl.ds(0, 7)], b0_send))
    bs[8:12] = dot_t(shapes_hi, coords[1])[0:64].reshape(4, 16, 128)
    br1[y % 4] = bs[8 + y % 4]
    for k in range(1, 4):
        d = (y % 4 + k) % 4
        send(bs.at[8 + d], br1.at[y % 4], b1_send, b1_recv, dev((y // 4) * 4 + d, z, c))
    drains.append(lambda: drain(br1.at[pl.ds(0, 3)], b1_send))
    bs[12:14] = dot_t(shapes_hi, coords[2])[64:96].reshape(2, 16, 128)
    br2[y % 2] = bs[12 + y % 2]
    d = 1 - y % 2
    send(bs.at[12 + d], br2.at[y % 2], b2_send, b2_recv, dev((y // 2) * 2 + d, z, c))
    drains.append(lambda: drain(br2.at[0], b2_send))
    m3[...] = dot_t(shapes_hi, coords[3])[96:112]

    def lookahead(n, d):
        piece = cl.at[zc, :, pl.ds(0, CL_AT[n + 1])]
        return piece, piece

    wait_lookahead = to_row(lookahead, lambda n, count: cl.at[pl.ds(0, count), :, pl.ds(0, CL_AT[n + 1])])

    arrange(1)

    def publish(s, modal):
        value = modal.astype(BF16)
        ny, nz = GROUPS[s]
        known[s][y % ny, z % nz, c] = value
        sv_ref[16 * s : 16 * s + 16, :] = value

    def permute(k_ref, kp):
        rows = kp.shape[0]
        each = rows // 8
        k32[0:rows] = k_ref[...].reshape(rows, 128).astype(F32)
        for j in range(8):
            kp[each * j : each * j + each] = k32[pl.ds(j, each, stride=8), :].astype(BF16)

    def spread_wide(s, during_first, during_second):
        ny, nz = GROUPS[s]
        k_ref = known[s]
        yi, zi = y % ny, z % nz
        y0, z0 = y - yi, z - zi
        (s1, r1, s2, s3, r3) = new_sems(5)
        r2 = new_sems(max(ny, nz) - 1)

        @pl.when(c == 0)
        def _():
            for k in range(1, ny):
                own = k_ref.at[yi, zi, 0]
                send(own, own, s1, r1, dev(y0 + (yi + k) % ny, z, 0))

        @pl.when(c == 1)
        def _():
            for k in range(1, nz):
                own = k_ref.at[yi, zi, 1]
                send(own, own, s1, r1, dev(y, z0 + (zi + k) % nz, 1))

        during_first()

        @pl.when(c == 0)
        def _():
            drain(k_ref.at[pl.ds(0, ny - 1), 0, 0], r1)
            own = k_ref.at[:, zi, 0]
            for k in range(1, nz):
                send(own, own, s2, r2[k - 1], dev(y, z0 + (zi + k) % nz, 0))
            send(own, own, s3, r3, dev(y, z, 1))

        @pl.when(c == 1)
        def _():
            drain(k_ref.at[0, pl.ds(0, nz - 1), 0], r1)
            own = k_ref.at[yi, :, 1]
            for k in range(1, ny):
                send(own, own, s2, r2[k - 1], dev(y0 + (yi + k) % ny, z, 1))
            send(own, own, s3, r3, dev(y, z, 0))

        during_second()

        def nearest(n):
            return sorted(range(1, n), key=lambda k: (min(k, n - k), k))

        @pl.when(c == 0)
        def _():
            for k in nearest(nz):
                piece = k_ref.at[:, (zi + nz - k) % nz, 0]
                drain(piece, r2[k - 1])
                send(piece, piece, s3, r3, dev(y, z, 1))

        @pl.when(c == 1)
        def _():
            for k in nearest(ny):
                piece = k_ref.at[(yi + ny - k) % ny, :, 1]
                drain(piece, r2[k - 1])
                send(piece, piece, s3, r3, dev(y, z, 0))

        drain(k_ref.at[:, :, 0], r3)

        def finish():
            @pl.when(c == 0)
            def _():
                drain(k_ref.at[pl.ds(0, ny - 1), 0, 0], s1)
                drain(k_ref.at[:, pl.ds(0, nz - 1), 0], s2)

            @pl.when(c == 1)
            def _():
                drain(k_ref.at[0, pl.ds(0, nz - 1), 0], s1)
                drain(k_ref.at[pl.ds(0, ny - 1), :, 0], s2)

            drain(k_ref.at[:, :, 0], s3)

        drains.append(finish)

    def spread_half(during):
        yi = y % 4
        (s0, s1, s3, r3) = new_sems(4)
        r1 = new_sems(4)
        own = k1.at[yi, z, c]
        for k in range(4):
            for i in range(1 if k == 0 else 0, NZ):
                send(own, own, s1 if k else s0, r1[k], dev(half + (y + k) % 4, (z + i) % NZ, c))
        during()
        drain(k1.at[0, pl.ds(0, 7), 0], r1[0])
        for k in (0, 1, 3, 2):
            piece = k1.at[(yi + 4 - k) % 4, :, c]
            if k:
                drain(piece, r1[k])
            send(piece, piece, s3, r3, dev(y, z, other))
        drain(k1.at[:, :, 0], r3)

        def finish():
            drain(k1.at[0, pl.ds(0, 7), 0], s0)
            drain(k1.at[pl.ds(0, 3), :, 0], s1)
            drain(k1.at[:, :, 0], s3)

        drains.append(finish)

    def spread_pair(during):
        yi = y % 2
        (s1, r1) = new_sems(2)
        own = kq.at[yi, zc, 0]

        def with_sums(n, d):
            piece = kq.at[yi, zc, pl.ds(0, 2 + n)]
            return piece, piece

        wait_row = to_row(with_sums, lambda n, count: kq.at[0, pl.ds(0, count), pl.ds(0, 2 + n)])
        for k in range(16):
            d = (zc + k) % 16
            send(own, own, s1, r1, dev(mate, d // 2, d % 2))
        during()
        wait_row()
        drain(kq.at[0, :, 0], r1)
        drains.append(lambda: drain(kq.at[0, :, 0], s1))

    def ancestors(block):
        first = k0[...].reshape(2048, 128)
        if block < 2:
            return first[1016 * block : 1016 * block + 1016]
        return jnp.concatenate([first[2032:], k1[...].reshape(1024, 128)[0:1000]], axis=0)

    drain(br0.at[pl.ds(0, 7)], b0_recv)
    publish(0, jnp.sum(br0[...], axis=0))

    def first_0():
        arrange(2)
        quad = mr[pl.ds(base4, 8), 48:64].astype(F32)
        two = mr[pl.ds(base5, 4), 64:80].astype(F32)
        chip = mr[pl.ds(base6, 2), 64:96].astype(F32)

        def part(block, at):
            return block[:, at : at + 8].reshape(-1, 128).astype(BF16)

        m456[0] = dot_t(part(quad, 8), part(quad, 0))
        m456[1] = dot_t(part(two, 8), part(two, 0))
        m456[2] = dot_t(part(chip, 8), part(chip, 16))

    def second_0():
        arrange(3)
        arrange(4)

    spread_wide(0, first_0, second_0)

    permute(k0, kp0)
    drain(br1.at[pl.ds(0, 3)], b1_recv)
    publish(1, jnp.sum(br1[...], axis=0) + dot(ct0[0], kp0[...]))

    def during_1():
        arrange(5)
        by_core(pass_on)
        arrange(6)
        pv[...] = dot(ct0[1:6].reshape(80, 2048), kp0[...]).reshape(5, 16, 128)

    spread_half(during_1)

    permute(k1, kp1)
    drain(br2.at[0], b2_recv)
    product = dot(ct1[...].reshape(80, 1024), kp1[...]) + pv[...].reshape(80, 128)

    def flush(keep):
        while len(drains) > keep:
            drains.pop(0)()

    def own_rows(s, at):
        return m456[s - 4, pl.ds(pl.multiple_of(at, 16), 16), :]

    blocks = (
        product[0:16] + jnp.sum(br2[...], axis=0),
        product[16:32] + m3[...],
        product[32:48] + own_rows(4, near4 * 16),
        product[48:64] + own_rows(5, near5 * 16),
        product[64:80] + own_rows(6, 64 + near6 * 16),
    )
    for n, value in enumerate(blocks):
        kq[y % 2, zc, n] = value.astype(BF16)
    sv_ref[32:48, :] = blocks[0].astype(BF16)

    def during_2():
        lq_copy.wait()
        lphi_copy.wait()
        acc[...] = dot(lq_ref[...], lphi_ref[...])
        cpl_copy.wait()
        by_core(wait_neighbours)
        for block in range(3):
            @pl.when((block + NX - x) % NX != 2)
            def _(block=block):
                acc[...] += dot_t(ancestors(block), cg[block])

        flush(1)

    spread_pair(during_2)

    wait_lookahead()
    above2 = kq[:, :, 0].reshape(512, 128)
    yi = y % 2
    pp3 = kq[yi, :, 1].reshape(256, 128).astype(F32)
    pp4 = kq[yi, pl.ds(base4, 8), 2].reshape(128, 128).astype(F32)
    pp5 = kq[yi, pl.ds(base5, 4), 3].reshape(64, 128).astype(F32)
    pp6 = kq[yi, pl.ds(base6, 2), 4].reshape(32, 128).astype(F32)
    c3 = cl[:, :, CL_AT[0] : CL_AT[1]].reshape(256, 512)
    c4 = cl[pl.ds(base4, 8), :, CL_AT[1] : CL_AT[2]].reshape(128, 768)
    c5 = cl[pl.ds(base5, 4), :, CL_AT[2] : CL_AT[3]].reshape(64, 896)
    c6 = cl[pl.ds(base6, 2), :, CL_AT[3] : CL_AT[4]].reshape(32, 1024)
    first = dot(jnp.concatenate([c3, c4[:, 0:512], c5[:, 0:512], c6[:, 0:512]], axis=0), above2)
    above3 = (pp3 + first[0:256]).astype(BF16)
    second = dot(jnp.concatenate([c4[:, 512:768], c5[:, 512:768], c6[:, 512:768]], axis=0), above3) + first[256:480]
    above4 = (pp4 + second[0:128]).astype(BF16)
    third = dot(jnp.concatenate([c5[:, 768:896], c6[:, 768:896]], axis=0), above4) + second[128:224]
    above5 = (pp5 + third[0:64]).astype(BF16)
    above6 = pp6 + third[64:96] + dot(c6[:, 896:960], above5)
    above6 = above6.astype(BF16)
    k3[...] = above3.reshape(16, 16, 128)
    k4[...] = above4.reshape(8, 16, 128)
    k5[...] = above5.reshape(4, 16, 128)
    k6[...] = above6.reshape(2, 16, 128)
    sv_ref[48:64, :] = k3[zc]
    sv_ref[64:80, :] = k4[near4]
    sv_ref[80:96, :] = k5[near5]
    sv_ref[96:112, :] = k6[near6]

    late = jnp.concatenate(
        [k1[...].reshape(1024, 128)[1000:], above2, above3, above4, above5, above6], axis=0
    )

    @pl.when(x != 1)
    def _():
        acc[...] += dot_t(late, cg[3])

    flush(0)
    by_core(wait_opposite)
    by_core(finish_gather)
    for block in range(NX):
        @pl.when((block + NX - x) % NX == 2)
        def _(block=block):
            acc[...] += dot_t(late if block == 3 else ancestors(block), cg[block])

    total = acc[...]
    live = lax.broadcasted_iota(jnp.int32, (COLS, LEAF), 1) < rows_ref[0]
    out_ref[...] = jnp.where(live, total, 0.0).astype(BF16)


def hand_over(values, leaf, values_out, leaf_out):
    leaf_out[...] = leaf[...]
    values_out[...] = values[...]


N_SEMS = 112


def body(sep_q, sep_phi, coupling, leaf_q, leaf_phi, leaf_coupling, leaf_rows):
    vmem = pl.BlockSpec(memory_space=pltpu.VMEM)
    hbm = pl.BlockSpec(memory_space=pl.ANY)
    block = (16, 128)
    scratch = [
        pltpu.VMEM((56, 128), BF16),
        pltpu.VMEM((8, 4064), BF16),
        pltpu.VMEM((128, 128), BF16),
        pltpu.VMEM((128, LEAF), BF16),
        pltpu.VMEM((1, 328704), BF16),
        pltpu.VMEM((CROWS + 8, 128), F32),
        pltpu.VMEM((128, 1024), BF16),
        pltpu.VMEM((128, 1024), F32),
        pltpu.VMEM((LEVELS - 1, 16, 2048), BF16),
        pltpu.VMEM((LEVELS - 2, 16, 1024), BF16),
        pltpu.VMEM((2048, 128), F32),
        pltpu.VMEM((2048, 128), BF16),
        pltpu.VMEM((1024, 128), BF16),
        pltpu.VMEM((NX, 1016, LEAF), BF16),
        pltpu.VMEM((16, 96, 128), BF16),
        pltpu.VMEM((16, 96, 128), BF16),
        pltpu.VMEM((14,) + block, F32),
        pltpu.VMEM((8,) + block, F32),
        pltpu.VMEM((4,) + block, F32),
        pltpu.VMEM((2,) + block, F32),
        pltpu.VMEM(block, F32),
        pltpu.VMEM((3, 128, 128), F32),
        pltpu.VMEM((16, 16, CL_AT[-1]), BF16),
    ]
    scratch += [pltpu.VMEM(group + (NC,) + block, BF16) for group in GROUPS[:2]]
    scratch += [pltpu.VMEM((2, 16, 5) + block, BF16)]
    scratch += [pltpu.VMEM((n,) + block, BF16) for n in (16, 8, 4, 2)]
    scratch += [
        pltpu.VMEM((LEVELS - 2, 16, 128), F32),
        pltpu.VMEM((COLS, LEAF), F32),
        pltpu.SemaphoreType.DMA((N_SEMS,)),
    ]
    values, leaf = pl.pallas_call(
        kernel,
        out_shape=(
            jax.ShapeDtypeStruct((16 * LEVELS, COLS), BF16),
            jax.ShapeDtypeStruct((COLS, LEAF), BF16),
        ),
        in_specs=[hbm, hbm, hbm, hbm, hbm, hbm, pl.BlockSpec(memory_space=pltpu.SMEM)],
        out_specs=(vmem, vmem),
        scratch_shapes=scratch,
        compiler_params=pltpu.CompilerParams(
            collective_id=0, has_side_effects=True, vmem_limit_bytes=56 * 1024 * 1024
        ),
        cost_estimate=pl.CostEstimate(flops=2_000_000_000, bytes_accessed=4_000_000, transcendentals=0),
    )(sep_q[0].T, sep_phi[0], coupling, leaf_q[0], leaf_phi[0], leaf_coupling[0], leaf_rows)
    values, leaf = pl.pallas_call(
        hand_over,
        out_shape=(
            jax.ShapeDtypeStruct((16 * LEVELS, COLS), BF16),
            jax.ShapeDtypeStruct((COLS, LEAF), BF16),
        ),
        in_specs=[vmem, vmem],
        out_specs=(vmem, vmem),
        compiler_params=pltpu.CompilerParams(vmem_limit_bytes=56 * 1024 * 1024),
    )(values, leaf)
    return values.T[None], leaf[None]


def solution(mesh):
    in_specs = (
        P("sub", "col", None),
        P("sub", None, None),
        P("sub", None),
        P("sub", "col", None),
        P("sub", None, None),
        P("sub", "col", None),
        P("sub"),
    )
    out_specs = (P("sub", "col", None), P("sub", "col", None))
    return jax.shard_map(body, mesh=mesh, in_specs=in_specs, out_specs=out_specs, check_vma=False)
```
